256 devices in a mesh: qrow: 16 (over x, z_hi, core), kcol: 16 (over y, z_lo).
Axes of the slice: x: 4, y: 4, z: 8 (z_hi: 2, z_lo: 4; z = z_hi * 4 + z_lo), core: 2. Of those that a mesh axis runs over, the one named last changes fastest.
Arguments:
- query: bfloat16 [32768, 512], P(('qrow', 'kcol')), may hold values from -6 to 6
- keys: bfloat16 [32768, 128], P(('kcol', 'qrow')), may hold values from -6 to 6
- values: bfloat16 [32768, 128], P(('kcol', 'qrow')), may hold values from -6 to 6
- out: bfloat16 [32768, 512], P(('qrow', 'kcol')), may hold values from -6 to 6
- out_grad: bfloat16 [32768, 512], P(('qrow', 'kcol')), may hold values from -0.59765625 to 0.59765625
- lse: float32 [4, 32768], P(None, ('qrow', 'kcol')), may hold values from 2.5 to 4.5
- cu_seqlens: int32 [7], replicated, may hold values from 0 to 32768, as said below
- tile_table: int32 [16, 16, 16], P('qrow', 'kcol'), may hold values from -1 to 15, as said below
Outputs:
- query_grad: bfloat16 [32768, 512], P(('qrow', 'kcol'))
- key_grad: bfloat16 [32768, 128], P(('kcol', 'qrow'))
- value_grad: bfloat16 [32768, 128], P(('kcol', 'qrow'))
The draws below stay inside these ranges and needn't reach their ends.
Inputs may be any that keep to these rules, and one draw needn't show every extreme that they name: cu_seqlens[0] = 0, cu_seqlens[6] = 32768, rising; every document holds 1024 to 16384 tokens, one exactly 1024 and one exactly 16384. tile_table[i, j] holds, in rising order, the codes of exactly those tiles of device (i, j) that contain a query row and a key row whose positions lie in one document with the key's position not after the query's, then -1 in the remaining entries.
All inputs are finite; a program needn't handle non-finite values.
Results may differ from the reference program's by a relative error of at most 0.0049.
Values may be sent and summed in bfloat16 or wider, within the bound.
A program may use at most 64 MiB of HBM per device.

```python
import math
import jax
import jax.numpy as jnp
from jax import lax

HEADS = 4
HEAD_DIM = 128
TOK_DEV = 128
TILE = 512
DOCS = 6
TOKENS = 32768
Q_BLOCK = 2048
K_BLOCK = 2048
K_TILES = 4
CAP = 16
DOC_MOST = 16384
DOC_LEAST = 1024
N_QROW = 16
N_KCOL = 16


def doc_bounds(key):
    weights = jax.random.randint(jax.random.fold_in(key, 11), (DOCS - 2,), 1, 64)
    spare_tokens = TOKENS - DOC_MOST - (DOCS - 1) * DOC_LEAST
    shares = spare_tokens * weights // jnp.sum(weights)
    shares = shares.at[0].add(spare_tokens - jnp.sum(shares))
    lengths = jnp.concatenate([jnp.array([DOC_MOST, DOC_LEAST], jnp.int32), (DOC_LEAST + shares).astype(jnp.int32)])
    doc_order = jax.random.permutation(jax.random.fold_in(key, 12), DOCS)
    lengths = lengths[doc_order]
    return jnp.concatenate([jnp.zeros((1,), jnp.int32), jnp.cumsum(lengths).astype(jnp.int32)])


def draw_cu_seqlens(key, part):
    bounds = doc_bounds(key)
    return bounds


def draw_tile_table(key, part):
    bounds = doc_bounds(key)
    q_tiles = TOK_DEV * N_KCOL // TILE
    k_tiles = TOK_DEV * N_QROW // TILE
    slots = q_tiles * k_tiles
    device_row = jnp.arange(N_QROW, dtype=jnp.int32)[:, None, None]
    device_col = jnp.arange(N_KCOL, dtype=jnp.int32)[None, :, None]
    slot_codes = jnp.arange(slots, dtype=jnp.int32)[None, None, :]
    query_tile = slot_codes // k_tiles * N_QROW + device_row
    key_tile = slot_codes % k_tiles * N_KCOL + device_col
    inner = bounds[1:-1]
    first_doc = jnp.sum((inner <= (query_tile * TILE)[..., None]).astype(jnp.int32), axis=-1)
    last_doc = jnp.sum((inner <= (key_tile * TILE + TILE - 1)[..., None]).astype(jnp.int32), axis=-1)
    live = (key_tile <= query_tile) & (first_doc <= last_doc)
    ranked = jnp.where(live, slot_codes, slots + slot_codes)
    ranked = jnp.sort(ranked, axis=-1)
    return jnp.where(ranked < slots, ranked, -1).astype(jnp.int32)


def block_scale(key, shape, shards, least, largest):
    gain, own = 1.0, jax.random.fold_in(key, 6)
    for position, shards_of in shards:
        steps = jnp.exp(jax.random.uniform(jax.random.fold_in(own, position), (shards_of,), jnp.float32, least / len(shards), largest / len(shards)))
        gain = gain * jnp.repeat(steps, shape[position] // shards_of).reshape([-1 if axis == position else 1 for axis in range(len(shape))])
    return gain


def normal_values(rng, shape, scale, most, cuts=(), kind=jnp.bfloat16):
    level = block_scale(rng, shape, cuts, -0.22, 0.18) if cuts else 1.0
    drawn = jax.random.normal(rng, shape, jnp.float32) * scale * level
    return jnp.minimum(jnp.maximum(drawn, -most), most).astype(kind)


def setup_inputs(seed: int = 0) -> dict:
    key_list = jax.random.split(jax.random.key(seed), 9)
    return {
        "query": normal_values(key_list[0], (TOKENS, HEADS * HEAD_DIM), 1.0, 6.0, ((0, 256),)),
        "keys": normal_values(key_list[1], (TOKENS, HEAD_DIM), 1.0, 6.0, ((0, 256),)),
        "values": normal_values(key_list[2], (TOKENS, HEAD_DIM), 1.0, 6.0, ((0, 256),)),
        "out": normal_values(key_list[3], (TOKENS, HEADS * HEAD_DIM), 1.0, 6.0, ((0, 256),)),
        "out_grad": normal_values(key_list[4], (TOKENS, HEADS * HEAD_DIM), 0.1, 0.59765625, ((0, 256),)),
        "lse": jnp.clip(2.5 + 2.0 * jax.random.uniform(key_list[5], (HEADS, TOKENS), jnp.float32) ** block_scale(key_list[5], (HEADS, TOKENS), ((1, 256),), -0.2, 0.2), 2.5, 4.5),
        "cu_seqlens": draw_cu_seqlens(jax.random.fold_in(key_list[8], 71), 0),
        "tile_table": draw_tile_table(jax.random.fold_in(key_list[8], 71), 0),
    }


def doc_of(positions, cu_seqlens):
    inner = cu_seqlens[1:-1]
    return lax.optimization_barrier(jnp.sum((inner[None, :] <= positions[:, None]).astype(jnp.int32), axis=1))

def low_copy(array):
    return lax.optimization_barrier(array.astype(jnp.bfloat16)).astype(jnp.float32)

def tile_grads(query_tile, grad_tile, key_tile, value_tile, lse_tile, delta_tile, query_pos, key_pos, cu_seqlens):
    row_count = query_tile.shape[0]
    scaling = 1.0 / math.sqrt(HEAD_DIM)
    query_heads = query_tile.astype(jnp.float32).reshape(row_count, HEADS, HEAD_DIM)
    grad_heads = grad_tile.astype(jnp.float32).reshape(row_count, HEADS, HEAD_DIM)
    key_wide = key_tile.astype(jnp.float32)
    value_wide = value_tile.astype(jnp.float32)
    scores = jnp.einsum('qhd,kd->hqk', query_heads, key_wide) * scaling
    same_doc = doc_of(query_pos, cu_seqlens)[:, None] == doc_of(key_pos, cu_seqlens)[None, :]
    allowed = same_doc & (key_pos[None, :] <= query_pos[:, None])
    weights = jnp.where(allowed[None], jnp.exp(scores - lse_tile[:, :, None]), jnp.float32(0.0))
    weights_low = low_copy(weights)
    dprobs = jnp.einsum('qhd,kd->hqk', grad_heads, value_wide)
    dscores = weights * (dprobs - delta_tile[:, :, None])
    dscores_low = low_copy(dscores)
    value_part = jnp.einsum('hqk,qhd->kd', weights_low, grad_heads)
    key_part = jnp.einsum('hqk,qhd->kd', dscores_low, query_heads) * scaling
    query_part = jnp.einsum('hqk,kd->qhd', dscores_low, key_wide).reshape(row_count, HEADS * HEAD_DIM) * scaling
    return (query_part, key_part, value_part)

def reference(query, keys, values, out, out_grad, lse, cu_seqlens, tile_table):
    deltas = lax.optimization_barrier(jnp.sum((out_grad.astype(jnp.float32) * out.astype(jnp.float32)).reshape(TOKENS, HEADS, HEAD_DIM), axis=2)).T
    tile_codes = tile_table.reshape(-1).astype(jnp.int32)
    numbers = jnp.arange(tile_codes.shape[0], dtype=jnp.int32)
    start_sums = (jnp.zeros((TOKENS, HEADS * HEAD_DIM), jnp.float32), jnp.zeros((TOKENS, HEAD_DIM), jnp.float32), jnp.zeros((TOKENS, HEAD_DIM), jnp.float32))

    def visit(totals, pair):
        number, tile_code = pair
        device = number // CAP
        row_dev = device // N_KCOL
        col_dev = device % N_KCOL
        q_tile = tile_code // K_TILES
        k_tile = tile_code % K_TILES
        q_start = (row_dev * Q_BLOCK + q_tile * TILE).astype(jnp.int32)
        k_start = (col_dev * K_BLOCK + k_tile * TILE).astype(jnp.int32)
        q_first = ((q_tile * N_QROW + row_dev) * TILE).astype(jnp.int32)
        k_first = ((k_tile * N_KCOL + col_dev) * TILE).astype(jnp.int32)

        def work(sums):
            query_sum, key_sum, value_sum = sums
            query_pos = q_first + jnp.arange(TILE, dtype=jnp.int32)
            key_pos = k_first + jnp.arange(TILE, dtype=jnp.int32)
            query_part, key_part, value_part = tile_grads(lax.dynamic_slice_in_dim(query, q_start, TILE, 0), lax.dynamic_slice_in_dim(out_grad, q_start, TILE, 0), lax.dynamic_slice_in_dim(keys, k_start, TILE, 0), lax.dynamic_slice_in_dim(values, k_start, TILE, 0), lax.dynamic_slice_in_dim(lse, q_start, TILE, 1), lax.dynamic_slice_in_dim(deltas, q_start, TILE, 1), query_pos, key_pos, cu_seqlens)
            query_sum = lax.dynamic_update_slice_in_dim(query_sum, lax.dynamic_slice_in_dim(query_sum, q_start, TILE, 0) + query_part, q_start, 0)
            key_sum = lax.dynamic_update_slice_in_dim(key_sum, lax.dynamic_slice_in_dim(key_sum, k_start, TILE, 0) + key_part, k_start, 0)
            value_sum = lax.dynamic_update_slice_in_dim(value_sum, lax.dynamic_slice_in_dim(value_sum, k_start, TILE, 0) + value_part, k_start, 0)
            return (query_sum, key_sum, value_sum)
        return (lax.cond(tile_code >= 0, work, lambda sums: sums, totals), None)
    final_sums, unused = lax.scan(visit, start_sums, (numbers, tile_codes))
    query_sum, key_sum, value_sum = final_sums
    return (query_sum.astype(jnp.bfloat16), key_sum.astype(jnp.bfloat16), value_sum.astype(jnp.bfloat16))
```

```python
import functools
import math

import jax
import jax.numpy as jnp
from jax import lax
from jax.experimental import pallas as pl
from jax.experimental.pallas import tpu as pltpu
from jax.sharding import PartitionSpec as P

MESH = pl.DeviceIdType.MESH
HEADS = 4
HEAD_DIM = 128
TILE = 512
SUB = 128
SCALE = 1.0 / math.sqrt(HEAD_DIM)
LOG2E = math.log2(math.e)
LANE = (((1,), (1,)), ((), ()))
ROW = (((0,), (0,)), ((), ()))
COLS = HEADS * SUB


def compute_kernel(
    cu_ref, q_ref, g_ref, st_ref, k_ref, v_ref, dq_ref, dk_ref, dv_ref, qh, gh, lse, delta, dqa, dka, dva
):
    row = lax.axis_index("qrow")
    col = lax.axis_index("kcol")
    y = col // 4
    part = col % 4
    for a in range(4):
        for h in range(HEADS):
            lanes = slice(h * SUB, (h + 1) * SUB)
            qh[a, lanes, :] = q_ref[a, :, lanes]
            gh[a, lanes, :] = g_ref[a, :, lanes]
            lse[a, :, lanes] = st_ref[a, h : h + 1, :]
            delta[a, :, lanes] = st_ref[a, HEADS + h : HEADS + h + 1, :]
    dka[...] = jnp.zeros_like(dka)
    dva[...] = jnp.zeros_like(dva)
    dqa[...] = jnp.zeros_like(dqa)

    def doc_start(pos):
        start = jnp.int32(0)
        for n in range(1, 6):
            start = jnp.where(cu_ref[n] <= pos, cu_ref[n], start)
        return start

    def tiles_before(tile):
        return tile // 16 * 4 + jnp.clip(tile % 16 - 4 * y, 0, 4)

    def query_part(a, carry):
        tile = a * 16 + row
        first = tile * TILE + part * SUB
        start = doc_start(first)
        last_start = doc_start(first + SUB - 1)
        low = tiles_before(start // TILE)
        high = tiles_before(tile + 1)
        qpos = first + lax.broadcasted_iota(jnp.int32, (1, SUB), 1)
        starts = jnp.zeros((1, SUB), jnp.int32)
        for n in range(1, 6):
            starts = jnp.where(cu_ref[n] <= qpos, cu_ref[n], starts)

        def unit(kt, masked):
            base = (kt // 4 * 16 + 4 * y + kt % 4) * TILE
            for part_k in range(2):
                rows = slice(part_k * 256, (part_k + 1) * 256)
                keys = k_ref[kt, rows, :]
                vals = v_ref[kt, rows, :]
                scores = lax.dot_general(keys, qh[a], LANE, preferred_element_type=jnp.float32)
                weights = jnp.exp2(scores * (SCALE * LOG2E) - lse[a])
                if masked:
                    kpos = base + part_k * 256 + lax.broadcasted_iota(jnp.int32, (256, SUB), 0)
                    allowed = (kpos >= starts) & (kpos <= qpos)
                    weights = jnp.concatenate(
                        [
                            jnp.where(allowed, weights[:, h * SUB : (h + 1) * SUB], 0.0)
                            for h in range(HEADS)
                        ],
                        axis=1,
                    )
                probs = lax.dot_general(vals, gh[a], LANE, preferred_element_type=jnp.float32)
                dscores = (weights * (probs - delta[a])).astype(jnp.bfloat16)
                dva[kt, rows, :] += jnp.dot(
                    weights.astype(jnp.bfloat16), gh[a], preferred_element_type=jnp.float32
                )
                dka[kt, rows, :] += jnp.dot(dscores, qh[a], preferred_element_type=jnp.float32)
                dqa[a] += lax.dot_general(dscores, keys, ROW, preferred_element_type=jnp.float32)

        def visit(kt, carry):
            base = (kt // 4 * 16 + 4 * y + kt % 4) * TILE
            full = (base + TILE - 1 <= first) & (last_start <= base)

            @pl.when(full)
            def _():
                unit(kt, False)

            @pl.when(jnp.logical_not(full))
            def _():
                unit(kt, True)

            return carry

        lax.fori_loop(low, high, visit, 0)
        return carry

    lax.fori_loop(0, 4, query_part, 0)
    for a in range(4):
        for h in range(HEADS):
            lanes = slice(h * SUB, (h + 1) * SUB)
            dq_ref[a, :, lanes] = (dqa[a, lanes, :] * SCALE).astype(jnp.bfloat16)

    def finish(kt, carry):
        dk_ref[kt] = (dka[kt] * SCALE).astype(jnp.bfloat16)
        dv_ref[kt] = dva[kt].astype(jnp.bfloat16)
        return carry

    lax.fori_loop(0, 16, finish, 0)


def compute(cu, q, g, st, k, v):
    vmem = pl.BlockSpec(memory_space=pltpu.VMEM)
    return pl.pallas_call(
        compute_kernel,
        out_shape=[
            jax.ShapeDtypeStruct((4, SUB, COLS), jnp.bfloat16),
            jax.ShapeDtypeStruct((16, TILE, HEAD_DIM), jnp.bfloat16),
            jax.ShapeDtypeStruct((16, TILE, HEAD_DIM), jnp.bfloat16),
        ],
        in_specs=[pl.BlockSpec(memory_space=pltpu.SMEM)] + [vmem] * 5,
        out_specs=[vmem] * 3,
        scratch_shapes=[
            pltpu.VMEM((4, COLS, HEAD_DIM), jnp.bfloat16),
            pltpu.VMEM((4, COLS, HEAD_DIM), jnp.bfloat16),
            pltpu.VMEM((4, 1, COLS), jnp.float32),
            pltpu.VMEM((4, 1, COLS), jnp.float32),
            pltpu.VMEM((4, COLS, HEAD_DIM), jnp.float32),
            pltpu.VMEM((16, TILE, HEAD_DIM), jnp.float32),
            pltpu.VMEM((16, TILE, HEAD_DIM), jnp.float32),
        ],
        compiler_params=pltpu.CompilerParams(vmem_limit_bytes=56 * 1024 * 1024),
        name="tiles",
    )(cu, q, g, st, k, v)


class Place:
    def __init__(self):
        row = lax.axis_index("qrow")
        col = lax.axis_index("kcol")
        self.x = row // 4
        self.core = row % 2
        self.y = col // 4
        self.z = row // 2 % 2 * 4 + col % 4

    def at(self, dx=0, dy=0, dz=0, flip=0):
        x = (self.x + dx + 4) % 4
        y = (self.y + dy + 4) % 4
        z = (self.z + dz + 8) % 8
        core = 1 - self.core if flip else self.core
        return (x * 4 + z // 4 * 2 + core, y * 4 + z % 4)

    def xs(self, dx):
        return (self.x + dx + 4) % 4

    def ys(self, dy):
        return (self.y + dy + 4) % 4

    def zs(self, dz):
        z = (self.z + dz + 8) % 8
        return z % 4 * 2 + z // 4


class Sender:
    def __init__(self, send_sem, recv_sem):
        self.send_sem = send_sem
        self.recv_sem = recv_sem
        self.sent = []

    def start(self, src, dst, device):
        number = len(self.sent)
        copy = pltpu.make_async_remote_copy(
            src_ref=src,
            dst_ref=dst,
            send_sem=self.send_sem.at[number],
            recv_sem=self.recv_sem.at[number],
            device_id=device,
            device_id_type=MESH,
        )
        copy.start()
        self.sent.append(copy)
        return copy

    def finish(self):
        for copy in self.sent:
            copy.wait_send()


def greet(devices):
    barrier = pltpu.get_barrier_semaphore()
    for device in devices:
        pl.semaphore_signal(barrier, inc=1, device_id=device, device_id_type=MESH)
    pl.semaphore_wait(barrier, len(devices))


GATHER_COPIES = 72
REDUCE_COPIES = 56


def gather_kernel(
    q_ref, g_ref, k_ref, v_ref, o_ref, lse_ref, qa, ga, ka, va, sta, stats, send_sem, recv_sem, own_sem
):
    me = Place()
    x, y, core = me.x, me.y, me.core
    greet(
        [
            me.at(dx=1),
            me.at(dx=2),
            me.at(dx=3),
            me.at(dy=1),
            me.at(dy=2),
            me.at(dy=3),
            me.at(dz=1),
            me.at(dz=-1),
            me.at(flip=1),
        ]
    )
    net = Sender(send_sem, recv_sem)
    here = me.zs(0)
    own = [
        pltpu.make_async_copy(k_ref, ka.at[x, here, core], own_sem.at[0]),
        pltpu.make_async_copy(v_ref, va.at[x, here, core], own_sem.at[1]),
        pltpu.make_async_copy(q_ref, qa.at[y], own_sem.at[2]),
        pltpu.make_async_copy(g_ref, ga.at[y], own_sem.at[3]),
    ]
    for copy in own:
        copy.start()

    v_up = [net.start(v_ref, va.at[x, here, core], me.at(dz=1))]
    v_down = [net.start(v_ref, va.at[x, here, core], me.at(dz=-1))]
    k_side = [net.start(k_ref, ka.at[x, here, core], me.at(dx=d)) for d in (1, 3, 2)]
    q_up = net.start(q_ref, qa.at[y], me.at(dy=1))
    g_down = net.start(g_ref, ga.at[y], me.at(dy=-1))
    q_down = net.start(q_ref, qa.at[y], me.at(dy=-1))
    g_up = net.start(g_ref, ga.at[y], me.at(dy=1))
    v_side = []
    v_far = []

    def spread(dz):
        slot = me.zs(dz)
        block = va.at[x, slot, core]
        v_side.append((dz, net.start(block, block, me.at(dx=1)), net.start(block, block, me.at(dx=-1))))

    def spread_far(number):
        dz, up, down = v_side[number]
        slot = me.zs(dz)
        up.wait_recv()
        down.wait_recv()
        if number % 2 == 0:
            block = va.at[me.xs(-1), slot, core]
            v_far.append(net.start(block, block, me.at(dx=1)))
        else:
            block = va.at[me.xs(1), slot, core]
            v_far.append(net.start(block, block, me.at(dx=-1)))

    for copy in own:
        copy.wait()
    spread(0)

    for h in range(HEADS):
        lanes = slice(h * SUB, (h + 1) * SUB)
        product = o_ref[:, lanes].astype(jnp.float32) * g_ref[:, lanes].astype(jnp.float32)
        stats[HEADS + h : HEADS + h + 1, :] = jnp.sum(product.T, axis=0, keepdims=True)
    stats[0:HEADS, :] = lse_ref[...] * LOG2E
    stat_own = pltpu.make_async_copy(stats, sta.at[y], own_sem.at[4])
    stat_own.start()
    stat_side = [net.start(stats, sta.at[y], me.at(dy=d)) for d in (1, 2, 3)]

    sibling = me.at(flip=1)
    mirrored = []

    def mirror(block):
        mirrored.append(net.start(block, block, sibling))

    def v_step(step):
        v_up[-1].wait_recv()
        v_down[-1].wait_recv()
        if step < 3:
            up = va.at[x, me.zs(-step), core]
            down = va.at[x, me.zs(step), core]
            v_up.append(net.start(up, up, me.at(dz=1)))
            v_down.append(net.start(down, down, me.at(dz=-1)))
        elif step == 3:
            up = va.at[x, me.zs(-3), core, 0:64]
            down = va.at[x, me.zs(3), core, 64:128]
            v_up.append(net.start(up, up, me.at(dz=1)))
            v_down.append(net.start(down, down, me.at(dz=-1)))
        if step < 4:
            spread(-step)
            spread(step)
        else:
            spread(4)

    v_step(1)
    for copy in k_side:
        copy.wait_recv()
    bundle = ka.at[:, here, core]
    k_up = [net.start(bundle, bundle, me.at(dz=1))]
    k_down = [net.start(bundle, bundle, me.at(dz=-1))]
    mirror(bundle)

    def k_step(step):
        k_up[-1].wait_recv()
        k_down[-1].wait_recv()
        if step < 3:
            up = ka.at[:, me.zs(-step), core]
            down = ka.at[:, me.zs(step), core]
            k_up.append(net.start(up, up, me.at(dz=1)))
            k_down.append(net.start(down, down, me.at(dz=-1)))
            mirror(up)
            mirror(down)
        elif step == 3:
            up = ka.at[0:2, me.zs(-3), core]
            down = ka.at[2:4, me.zs(3), core]
            k_up.append(net.start(up, up, me.at(dz=1)))
            k_down.append(net.start(down, down, me.at(dz=-1)))
            mirror(ka.at[:, me.zs(-3), core])
            mirror(ka.at[:, me.zs(3), core])
        else:
            mirror(ka.at[:, me.zs(4), core])

    v_step(2)
    q_up.wait_recv()
    block = qa.at[me.ys(-1)]
    q_far = net.start(block, block, me.at(dy=1))
    g_down.wait_recv()
    block = ga.at[me.ys(1)]
    g_far = net.start(block, block, me.at(dy=-1))
    v_step(3)
    k_step(1)
    spread_far(0)
    spread_far(1)
    spread_far(2)
    v_step(4)
    mirror(va.at[x, :, core])
    k_step(2)
    spread_far(3)
    spread_far(4)
    spread_far(5)
    k_step(3)
    spread_far(6)
    spread_far(7)
    mirror(va.at[me.xs(1), :, core])
    mirror(va.at[me.xs(-1), :, core])
    k_step(4)
    for copy in v_far:
        copy.wait_recv()
    mirror(va.at[me.xs(2), :, core])
    for copy in [q_down, g_up, q_far, g_far] + stat_side + mirrored:
        copy.wait_recv()
    stat_own.wait()
    net.finish()


def gather(q, g, k, v, o, lse):
    vmem = pl.BlockSpec(memory_space=pltpu.VMEM)
    anywhere = pl.BlockSpec(memory_space=pl.ANY)
    return pl.pallas_call(
        gather_kernel,
        out_shape=[
            jax.ShapeDtypeStruct((4, SUB, COLS), jnp.bfloat16),
            jax.ShapeDtypeStruct((4, SUB, COLS), jnp.bfloat16),
            jax.ShapeDtypeStruct((4, 8, 2, SUB, HEAD_DIM), jnp.bfloat16),
            jax.ShapeDtypeStruct((4, 8, 2, SUB, HEAD_DIM), jnp.bfloat16),
            jax.ShapeDtypeStruct((4, 2 * HEADS, SUB), jnp.float32),
        ],
        in_specs=[vmem] * 6,
        out_specs=[anywhere] * 5,
        scratch_shapes=[
            pltpu.VMEM((2 * HEADS, SUB), jnp.float32),
            pltpu.SemaphoreType.DMA((GATHER_COPIES,)),
            pltpu.SemaphoreType.DMA((GATHER_COPIES,)),
            pltpu.SemaphoreType.DMA((5,)),
        ],
        compiler_params=pltpu.CompilerParams(
            collective_id=0, has_side_effects=True, vmem_limit_bytes=16 * 1024 * 1024
        ),
        name="gather",
    )(q, g, k, v, o, lse)


def reduce_kernel(
    dq_ref,
    dk_ref,
    dv_ref,
    dq_out,
    dk_out,
    dv_out,
    k_own,
    v_own,
    k_in,
    v_in,
    q_in,
    kx_send,
    kx_in,
    kz_send,
    kz_in,
    vz_send,
    vz_in,
    vx_send,
    vx_in,
    q_own,
    send_sem,
    recv_sem,
    own_sem,
):
    me = Place()
    x, y, core = me.x, me.y, me.core
    other = 1 - core
    sibling = me.at(flip=1)
    own = [
        pltpu.make_async_copy(dk_ref.at[:, :, core], k_own, own_sem.at[0]),
        pltpu.make_async_copy(dv_ref.at[:, :, core], v_own, own_sem.at[1]),
        pltpu.make_async_copy(dq_ref.at[y], q_own, own_sem.at[2]),
    ]
    for copy in own:
        copy.start()
    peers = [me.at(dx=d) for d in (1, 2, 3)] + [me.at(dy=d) for d in (1, 2, 3)]
    peers += [me.at(dz=d) for d in range(1, 8)] + [sibling]
    greet(peers)
    net = Sender(send_sem, recv_sem)
    f32 = jnp.float32
    bf16 = jnp.bfloat16

    v_pair = {}
    k_pair = {}

    def pair_v(dz):
        v_pair[dz] = net.start(dv_ref.at[:, me.zs(dz), other], v_in.at[:, me.zs(dz)], sibling)

    def pair_k(dx):
        k_pair[dx] = net.start(dk_ref.at[me.xs(dx), :, other], k_in.at[me.xs(dx)], sibling)

    pair_v(4)
    pair_k(2)
    pair_v(3)
    pair_v(-3)
    pair_k(1)
    pair_v(2)
    pair_v(-2)
    pair_k(-1)
    pair_v(1)
    pair_v(-1)
    pair_k(0)
    pair_v(0)
    q_side = [net.start(dq_ref.at[me.ys(d)], q_in.at[d - 1], me.at(dy=d)) for d in (1, 3, 2)]
    for copy in own:
        copy.wait()

    def v_sum(dz, rows):
        slot = me.zs(dz)
        return v_own[rows, slot].astype(f32) + v_in[rows, slot].astype(f32)

    def k_sum(dx, rows):
        slot = me.xs(dx)
        return k_own[slot, rows].astype(f32) + k_in[slot, rows].astype(f32)

    low, high, both = slice(0, 2), slice(2, 4), slice(0, 4)
    first, second = slice(0, 4), slice(4, 8)

    v_pair[4].wait_recv()
    vz_send[0, 0, low] = v_sum(4, low).astype(bf16)
    vz_send[1, 0, high] = v_sum(4, high).astype(bf16)
    v_up = [net.start(vz_send.at[0, 0, low], vz_in.at[0, 0, low], me.at(dz=1))]
    v_down = [net.start(vz_send.at[1, 0, high], vz_in.at[1, 0, high], me.at(dz=-1))]

    k_pair[2].wait_recv()
    kx_send[0, 0] = k_sum(2, first).astype(bf16)
    kx_send[1, 0] = k_sum(2, second).astype(bf16)
    kx_up = [net.start(kx_send.at[0, 0], kx_in.at[0, 0], me.at(dx=1))]
    kx_down = [net.start(kx_send.at[1, 0], kx_in.at[1, 0], me.at(dx=-1))]

    def v_step(step):
        dz = 4 - step
        v_pair[dz].wait_recv()
        v_pair[-dz].wait_recv()
        v_up[-1].wait_recv()
        v_down[-1].wait_recv()
        if step == 1:
            vz_send[0, 1, low] = (v_sum(dz, low) + vz_in[0, 0, low].astype(f32)).astype(bf16)
            vz_send[0, 1, high] = v_sum(dz, high).astype(bf16)
            vz_send[1, 1, low] = v_sum(-dz, low).astype(bf16)
            vz_send[1, 1, high] = (v_sum(-dz, high) + vz_in[1, 0, high].astype(f32)).astype(bf16)
        else:
            vz_send[0, step] = (v_sum(dz, both) + vz_in[0, step - 1].astype(f32)).astype(bf16)
            vz_send[1, step] = (v_sum(-dz, both) + vz_in[1, step - 1].astype(f32)).astype(bf16)
        v_up.append(net.start(vz_send.at[0, step], vz_in.at[0, step], me.at(dz=1)))
        v_down.append(net.start(vz_send.at[1, step], vz_in.at[1, step], me.at(dz=-1)))

    k_pair[1].wait_recv()
    k_pair[-1].wait_recv()
    kx_send[0, 1] = k_sum(1, second).astype(bf16)
    kx_send[1, 1] = k_sum(-1, first).astype(bf16)
    kx_up.append(net.start(kx_send.at[0, 1], kx_in.at[0, 1], me.at(dx=1)))
    kx_down.append(net.start(kx_send.at[1, 1], kx_in.at[1, 1], me.at(dx=-1)))
    v_step(1)
    kx_up[0].wait_recv()
    kx_down[0].wait_recv()
    kx_send[0, 2] = (k_sum(1, first) + kx_in[0, 0].astype(f32)).astype(bf16)
    kx_send[1, 2] = (k_sum(-1, second) + kx_in[1, 0].astype(f32)).astype(bf16)
    kx_up.append(net.start(kx_send.at[0, 2], kx_in.at[0, 2], me.at(dx=1)))
    kx_down.append(net.start(kx_send.at[1, 2], kx_in.at[1, 2], me.at(dx=-1)))
    v_step(2)
    v_step(3)

    k_pair[0].wait_recv()
    for copy in (kx_up[1], kx_up[2], kx_down[1], kx_down[2]):
        copy.wait_recv()
    k_total = k_sum(0, first) + kx_in[0, 2].astype(f32) + kx_in[1, 1].astype(f32)
    kz_send[0:4] = k_total.astype(bf16)
    k_total = k_sum(0, second) + kx_in[0, 1].astype(f32) + kx_in[1, 2].astype(f32)
    kz_send[4:8] = k_total.astype(bf16)
    kz = [net.start(kz_send.at[me.zs(d)], kz_in.at[d - 1], me.at(dz=d)) for d in (4, 3, 5, 2, 6, 1, 7)]

    v_pair[0].wait_recv()
    v_up[3].wait_recv()
    v_down[3].wait_recv()
    vx_send[...] = (
        v_sum(0, both) + vz_in[0, 3].astype(f32) + vz_in[1, 3].astype(f32)
    ).astype(bf16)
    vx = [net.start(vx_send.at[me.xs(d)], vx_in.at[d - 1], me.at(dx=d)) for d in (1, 3, 2)]

    for copy in q_side:
        copy.wait_recv()
    total = q_own[...].astype(f32)
    for n in range(3):
        total += q_in[n].astype(f32)
    dq_out[...] = total.astype(bf16)
    for copy in kz:
        copy.wait_recv()
    total = kz_send[me.zs(0)].astype(f32)
    for n in range(7):
        total += kz_in[n].astype(f32)
    dk_out[...] = total.astype(bf16)
    for copy in vx:
        copy.wait_recv()
    total = vx_send[x].astype(f32)
    for n in range(3):
        total += vx_in[n].astype(f32)
    dv_out[...] = total.astype(bf16)
    net.finish()


def reduce(dq, dk, dv):
    vmem = pl.BlockSpec(memory_space=pltpu.VMEM)
    anywhere = pl.BlockSpec(memory_space=pl.ANY)
    bf16 = jnp.bfloat16
    block = (SUB, HEAD_DIM)
    return pl.pallas_call(
        reduce_kernel,
        out_shape=[
            jax.ShapeDtypeStruct((SUB, COLS), bf16),
            jax.ShapeDtypeStruct(block, bf16),
            jax.ShapeDtypeStruct(block, bf16),
        ],
        in_specs=[anywhere] * 3,
        out_specs=[vmem] * 3,
        scratch_shapes=[
            pltpu.VMEM((4, 8) + block, bf16),
            pltpu.VMEM((4, 8) + block, bf16),
            pltpu.VMEM((4, 8) + block, bf16),
            pltpu.VMEM((4, 8) + block, bf16),
            pltpu.VMEM((3, SUB, COLS), bf16),
            pltpu.VMEM((2, 3, 4) + block, bf16),
            pltpu.VMEM((2, 3, 4) + block, bf16),
            pltpu.VMEM((8,) + block, bf16),
            pltpu.VMEM((7,) + block, bf16),
            pltpu.VMEM((2, 4, 4) + block, bf16),
            pltpu.VMEM((2, 4, 4) + block, bf16),
            pltpu.VMEM((4,) + block, bf16),
            pltpu.VMEM((3,) + block, bf16),
            pltpu.VMEM((SUB, COLS), bf16),
            pltpu.SemaphoreType.DMA((REDUCE_COPIES,)),
            pltpu.SemaphoreType.DMA((REDUCE_COPIES,)),
            pltpu.SemaphoreType.DMA((3,)),
        ],
        compiler_params=pltpu.CompilerParams(
            collective_id=1, has_side_effects=True, vmem_limit_bytes=32 * 1024 * 1024
        ),
        name="reduce",
    )(dq, dk, dv)


def per_device(query, keys, values, out, out_grad, lse, cu_seqlens, tile_table):
    q, g, k, v, st = gather(query, out_grad, keys, values, out, lse)
    tiles = (16, TILE, HEAD_DIM)
    dq, dk, dv = compute(cu_seqlens, q, g, st, k.reshape(tiles), v.reshape(tiles))
    blocks = (4, 8, 2, SUB, HEAD_DIM)
    return reduce(dq, dk.reshape(blocks), dv.reshape(blocks))


def solution(mesh):
    placed = (
        P(("qrow", "kcol"), None),
        P(("kcol", "qrow"), None),
        P(("kcol", "qrow"), None),
        P(("qrow", "kcol"), None),
        P(("qrow", "kcol"), None),
        P(None, ("qrow", "kcol")),
        P(),
        P("qrow", "kcol", None),
    )
    return jax.shard_map(
        per_device,
        mesh=mesh,
        in_specs=placed,
        out_specs=(P(("qrow", "kcol"), None), P(("kcol", "qrow"), None), P(("kcol", "qrow"), None)),
        check_vma=False,
    )
```

```python
import math

import jax
import jax.numpy as jnp
from jax import lax
from jax.experimental import pallas as pl
from jax.experimental.pallas import tpu as pltpu
from jax.sharding import PartitionSpec as P

MESH = pl.DeviceIdType.MESH
HEADS = 4
HEAD_DIM = 128
TILE = 512
SUB = 128
COLS = HEADS * SUB
TOKENS = 32768
SCALE = 1.0 / math.sqrt(HEAD_DIM)
LOG2E = math.log2(math.e)
LANE = (((1,), (1,)), ((), ()))
ROW = (((0,), (0,)), ((), ()))
BF16 = jnp.bfloat16
F32 = jnp.float32
VMEM = pl.BlockSpec(memory_space=pltpu.VMEM)
ANY = pl.BlockSpec(memory_space=pl.ANY)


class Place:
    def __init__(self):
        row = lax.axis_index("qrow")
        col = lax.axis_index("kcol")
        self.x = row // 4
        self.core = row % 2
        self.y = col // 4
        self.z = row // 2 % 2 * 4 + col % 4

    def at(self, dx=0, dy=0, dz=0, flip=0):
        x = (self.x + dx + 4) % 4
        y = (self.y + dy + 4) % 4
        z = (self.z + dz + 8) % 8
        core = 1 - self.core if flip else self.core
        return (x * 4 + z // 4 * 2 + core, y * 4 + z % 4)

    def xs(self, dx):
        return (self.x + dx + 4) % 4

    def ys(self, dy):
        return (self.y + dy + 4) % 4

    def zs(self, dz):
        z = (self.z + dz + 8) % 8
        return z % 4 * 2 + z // 4


class Sender:
    def __init__(self, send_sem, recv_sem):
        self.send_sem = send_sem
        self.recv_sem = recv_sem
        self.sent = []

    def start(self, src, dst, device):
        number = len(self.sent)
        copy = pltpu.make_async_remote_copy(
            src_ref=src,
            dst_ref=dst,
            send_sem=self.send_sem.at[number],
            recv_sem=self.recv_sem.at[number],
            device_id=device,
            device_id_type=MESH,
        )
        copy.start()
        self.sent.append(copy)
        return copy

    def finish(self):
        for copy in self.sent:
            copy.wait_send()


def greet(devices):
    barrier = pltpu.get_barrier_semaphore()
    for device in devices:
        pl.semaphore_signal(barrier, inc=1, device_id=device, device_id_type=MESH)
    pl.semaphore_wait(barrier, len(devices))


def load(pairs, sems):
    copies = [pltpu.make_async_copy(src, dst, sems.at[n]) for n, (src, dst) in enumerate(pairs)]
    for copy in copies:
        copy.start()
    return copies


def gather_kernel(
    q_ref, g_ref, k_ref, v_ref, o_ref, lse_ref, qa, ga, ka, va, sta, g_in, o_in, lse_in, stats,
    send_q, recv_q, send_s, recv_s, send_m, recv_m, send_b, recv_b, own_sem
):
    me = Place()
    x, y, core = me.x, me.y, me.core
    here = me.zs(0)
    sibling = me.at(flip=1)
    own = load(
        [
            (k_ref, ka.at[x, here]),
            (v_ref, va.at[x, here]),
            (q_ref, qa.at[core, y]),
            (g_ref, ga.at[core, y]),
            (g_ref, g_in),
            (o_ref, o_in),
            (lse_ref, lse_in),
        ],
        own_sem,
    )
    greet(
        [me.at(dx=d) for d in (1, 2, 3)]
        + [me.at(dy=d) for d in (1, 2, 3)]
        + [me.at(dy=d, flip=1) for d in (1, 2, 3)]
        + [me.at(dz=1), me.at(dz=-1), sibling]
    )
    net = Sender(send_b, recv_b)
    rows = Sender(send_q, recv_q)
    small = Sender(send_s, recv_s)
    pair = Sender(send_m, recv_m)
    up = net.start(v_ref, va.at[x, here], me.at(dz=1))
    down = net.start(v_ref, va.at[x, here], me.at(dz=-1))
    k_side = [net.start(k_ref, ka.at[x, here], me.at(dx=d)) for d in (1, 3, 2)]
    v_side = [net.start(v_ref, va.at[x, here], me.at(dx=d)) for d in (1, 3, 2)]
    q_rows = {}
    for d in (1, 3, 2):
        q_rows[d] = (
            rows.start(q_ref, qa.at[core, y], me.at(dy=d)),
            rows.start(g_ref, ga.at[core, y], me.at(dy=d)),
        )
    pair.start(q_ref, qa.at[core, y], sibling)
    pair.start(g_ref, ga.at[core, y], sibling)

    def spread(dz):
        block = va.at[x, me.zs(dz)]
        for d in (1, 3, 2):
            v_side.append(net.start(block, block, me.at(dx=d)))

    def mirror(d):
        slot = me.ys(-d)
        for copy, block in zip(q_rows[d], (qa.at[core, slot], ga.at[core, slot])):
            copy.wait_recv()
            pair.start(block, block, sibling)

    halves = (slice(0, 2), slice(2, 4))
    own[0].wait()
    for copy in k_side:
        copy.wait_recv()
    k_up = []
    k_down = []
    for half in halves:
        block = ka.at[half, here]
        k_up.append(net.start(block, block, me.at(dz=1)))
        k_down.append(net.start(block, block, me.at(dz=-1)))

    def k_step(step):
        for n, half in enumerate(halves):
            if step < 4 or n == 0:
                k_up[n].wait_recv()
            if step < 3 or (step == 3 and n == 0):
                block = ka.at[half, me.zs(-step)]
                k_up[n] = net.start(block, block, me.at(dz=1))
            if step < 4 or n == 1:
                k_down[n].wait_recv()
            if step < 3 or (step == 3 and n == 1):
                block = ka.at[half, me.zs(step)]
                k_down[n] = net.start(block, block, me.at(dz=-1))

    def v_step(up, down, step):
        up.wait_recv()
        down.wait_recv()
        if step < 4:
            part = (slice(0, SUB), slice(0, SUB)) if step < 3 else (slice(0, 64), slice(64, SUB))
            block = va.at[x, me.zs(-step), part[0]]
            up = net.start(block, block, me.at(dz=1))
            block = va.at[x, me.zs(step), part[1]]
            down = net.start(block, block, me.at(dz=-1))
            spread(-step)
            spread(step)
        else:
            spread(4)
        return up, down

    up, down = v_step(up, down, 1)
    for copy in own[4:]:
        copy.wait()
    for h in range(HEADS):
        lanes = slice(h * SUB, (h + 1) * SUB)
        product = o_in[:, lanes].astype(F32) * g_in[:, lanes].astype(F32)
        stats[HEADS + h : HEADS + h + 1, :] = jnp.sum(product.T, axis=0, keepdims=True)
    stats[0:HEADS, :] = lse_in[...]
    stat_own = pltpu.make_async_copy(stats, sta.at[core, y], own_sem.at[7])
    stat_own.start()
    k_step(1)
    up, down = v_step(up, down, 2)
    for d in (1, 3, 2):
        small.start(stats, sta.at[core, y], me.at(dy=d))
        small.start(stats, sta.at[core, y], me.at(dy=d, flip=1))
    small.start(stats, sta.at[core, y], sibling)
    k_step(2)
    up, down = v_step(up, down, 3)
    mirror(1)
    mirror(3)
    k_step(3)
    v_step(up, down, 4)
    mirror(2)
    k_step(4)
    for copy in v_side + small.sent + pair.sent:
        copy.wait_recv()
    own[1].wait()
    own[2].wait()
    own[3].wait()
    stat_own.wait()
    for sender in (net, rows, small, pair):
        sender.finish()


def gather(q, g, k, v, o, lse):
    dma = pltpu.SemaphoreType.DMA
    return pl.pallas_call(
        gather_kernel,
        out_shape=[
            jax.ShapeDtypeStruct((2, 4, SUB, COLS), BF16),
            jax.ShapeDtypeStruct((2, 4, SUB, COLS), BF16),
            jax.ShapeDtypeStruct((4, 8, SUB, HEAD_DIM), BF16),
            jax.ShapeDtypeStruct((4, 8, SUB, HEAD_DIM), BF16),
            jax.ShapeDtypeStruct((2, 4, 2 * HEADS, SUB), F32),
        ],
        in_specs=[ANY] * 6,
        out_specs=[ANY] * 5,
        scratch_shapes=[
            pltpu.VMEM((SUB, COLS), BF16),
            pltpu.VMEM((SUB, COLS), BF16),
            pltpu.VMEM((HEADS, SUB), F32),
            pltpu.VMEM((2 * HEADS, SUB), F32),
            dma((6,)),
            dma((6,)),
            dma((7,)),
            dma((7,)),
            dma((8,)),
            dma((8,)),
            dma((49,)),
            dma((49,)),
            dma((8,)),
        ],
        compiler_params=pltpu.CompilerParams(
            collective_id=0, has_side_effects=True, vmem_limit_bytes=63 * 1024 * 1024
        ),
        name="gather",
    )(q, g, k, v, o, lse)


def tiles_kernel(
    cu_ref, q_hbm, g_hbm, st_hbm, k_hbm, v_hbm, dq_hbm, dk_hbm, dv_hbm, q_ref, g_ref, st_ref, k_ref, v_ref, dq_ref, dk_ref, dv_ref,
    qh, gh, feats, dqa, dka, dva, in_sem, out_sem
):
    row = lax.axis_index("qrow")
    col = lax.axis_index("kcol")
    y = col // 4
    part = col % 4
    core = row % 2
    row0 = row - core
    loads = load([(st_hbm, st_ref), (q_hbm, q_ref), (g_hbm, g_ref), (k_hbm, k_ref), (v_hbm, v_ref)], in_sem)
    lane = lax.broadcasted_iota(jnp.int32, (1, SUB), 1)
    sub = lax.broadcasted_iota(jnp.int32, (SUB, 1), 0)
    low_cu = jnp.zeros((1, SUB), jnp.int32) + TOKENS
    high_cu = jnp.zeros((1, SUB), jnp.int32)
    for n in range(6):
        low_cu = jnp.where(lane == n, cu_ref[n], low_cu)
        high_cu = jnp.where(lane == n, cu_ref[n + 1], high_cu)
    ones = (lane >= 8) & (lane < 11)

    def key_base(kt):
        return (kt // 4 * 16 + 4 * y + kt % 4) * TILE + core * SUB

    def clear(kt, carry):
        dka[kt] = jnp.zeros((2 * SUB, HEAD_DIM), F32)
        dva[kt] = jnp.zeros((2 * SUB, HEAD_DIM), F32)
        for zh in range(2):
            pos = key_base(kt) + zh * 2 * SUB + sub
            feats[kt, zh * SUB : (zh + 1) * SUB, :] = (((pos >= low_cu) & (pos < high_cu)) | ones).astype(F32).astype(BF16)
        return carry

    lax.fori_loop(0, 16, clear, 0)
    dqa[...] = jnp.zeros_like(dqa)

    def pieces(vec):
        out = jnp.zeros((SUB, SUB), F32)
        rest = vec
        for n in range(3):
            piece = rest.astype(BF16).astype(F32)
            rest = rest - piece
            out = jnp.where(lane == 8 + n, piece, out)
        return out

    for copy in loads[:3]:
        copy.wait()

    def stack(a, carry):
        for c in range(2):
            qpos = (a * 16 + row0 + c) * TILE + part * SUB + sub
            inside = (qpos >= low_cu) & (qpos < high_cu)
            doc_feat = jnp.where(inside | (lane >= 6), 0.0, -16384.0)
            stat = st_ref[c, a].T
            for h in range(HEADS):
                lanes = slice(h * SUB, (h + 1) * SUB)
                to = slice(c * COLS + h * SUB, c * COLS + (h + 1) * SUB)
                qh[a, to, 0:128] = q_ref[c, a, :, lanes]
                gh[a, to, 0:128] = g_ref[c, a, :, lanes]
                qh[a, to, 128:256] = (doc_feat + pieces(stat[:, h : h + 1] * (-1.0 / SCALE))).astype(BF16)
                gh[a, to, 128:256] = pieces(-stat[:, HEADS + h : HEADS + h + 1]).astype(BF16)
        return carry

    lax.fori_loop(0, 4, stack, 0)
    for copy in loads[3:]:
        copy.wait()

    def doc_start(pos):
        start = jnp.int32(0)
        for n in range(1, 6):
            start = jnp.where(cu_ref[n] <= pos, cu_ref[n], start)
        return start

    def tiles_before(tile):
        return tile // 16 * 4 + jnp.clip(tile % 16 - 4 * y, 0, 4)

    def query_part(a, carry):
        tile = a * 16 + row0
        first = tile * TILE + part * SUB
        low = tiles_before(doc_start(first) // TILE)
        high = tiles_before(tile + 2)

        def unit(kt, masked):
            keys = k_ref[kt]
            vals = v_ref[kt]
            feat = feats[kt]
            scores = lax.dot_general(
                jnp.concatenate([keys, feat], axis=1), qh[a], LANE, preferred_element_type=F32
            )
            weights = jnp.exp2(scores * (SCALE * LOG2E))
            if masked:
                kpos = lax.broadcasted_iota(jnp.int32, (2 * SUB, SUB), 0)
                kpos = jnp.where(kpos >= SUB, kpos + SUB, kpos) + key_base(kt)
                keep = [kpos <= first + lane, kpos <= first + TILE + lane]
                weights = jnp.concatenate(
                    [
                        jnp.where(keep[n // HEADS], weights[:, n * SUB : (n + 1) * SUB], 0.0)
                        for n in range(2 * HEADS)
                    ],
                    axis=1,
                )
            probs = lax.dot_general(
                jnp.concatenate([vals, feat], axis=1), gh[a], LANE, preferred_element_type=F32
            )
            dscores = (weights * probs).astype(BF16)
            dva[kt] += jnp.dot(weights.astype(BF16), gh[a, :, 0:128], preferred_element_type=F32)
            dka[kt] += jnp.dot(dscores, qh[a, :, 0:128], preferred_element_type=F32)
            dqa[a] += lax.dot_general(keys, dscores, ROW, preferred_element_type=F32)

        def visit(kt, carry):
            full = (kt // 4 * 16 + 4 * y + kt % 4) < tile

            @pl.when(full)
            def _():
                unit(kt, False)

            @pl.when(jnp.logical_not(full))
            def _():
                unit(kt, True)

            return carry

        lax.fori_loop(low, high, visit, 0)
        return carry

    lax.fori_loop(0, 4, query_part, 0)
    stores = []
    for b in range(4):
        rows = pl.ds(4 * b, 4)
        for kt in range(4 * b, 4 * b + 4):
            dk_ref[kt] = (dka[kt] * SCALE).astype(BF16)
            dv_ref[kt] = dva[kt].astype(BF16)
        for src, dst in ((dk_ref, dk_hbm), (dv_ref, dv_hbm)):
            copy = pltpu.make_async_copy(src.at[rows], dst.at[rows], out_sem.at[len(stores)])
            copy.start()
            stores.append(copy)
    for c in range(2):
        for a in range(4):
            for h in range(HEADS):
                lanes = slice(h * SUB, (h + 1) * SUB)
                to = slice(c * COLS + h * SUB, c * COLS + (h + 1) * SUB)
                dq_ref[c, a, :, lanes] = (dqa[a, :, to].T * SCALE).astype(BF16)
        copy = pltpu.make_async_copy(dq_ref.at[c], dq_hbm.at[c], out_sem.at[len(stores)])
        copy.start()
        stores.append(copy)
    for copy in stores:
        copy.wait()


def tiles(cu, q, g, st, k, v):
    keys = (16, 2 * SUB, HEAD_DIM)
    rows = (2, 4, SUB, COLS)
    return pl.pallas_call(
        tiles_kernel,
        out_shape=[
            jax.ShapeDtypeStruct(rows, BF16),
            jax.ShapeDtypeStruct(keys, BF16),
            jax.ShapeDtypeStruct(keys, BF16),
        ],
        in_specs=[pl.BlockSpec(memory_space=pltpu.SMEM)] + [ANY] * 5,
        out_specs=[ANY] * 3,
        scratch_shapes=[
            pltpu.VMEM(rows, BF16),
            pltpu.VMEM(rows, BF16),
            pltpu.VMEM((2, 4, 2 * HEADS, SUB), F32),
            pltpu.VMEM(keys, BF16),
            pltpu.VMEM(keys, BF16),
            pltpu.VMEM(rows, BF16),
            pltpu.VMEM(keys, BF16),
            pltpu.VMEM(keys, BF16),
            pltpu.VMEM((4, 2 * COLS, 256), BF16),
            pltpu.VMEM((4, 2 * COLS, 256), BF16),
            pltpu.VMEM(keys, BF16),
            pltpu.VMEM((4, HEAD_DIM, 2 * COLS), F32),
            pltpu.VMEM(keys, F32),
            pltpu.VMEM(keys, F32),
            pltpu.SemaphoreType.DMA((5,)),
            pltpu.SemaphoreType.DMA((10,)),
        ],
        compiler_params=pltpu.CompilerParams(vmem_limit_bytes=63 * 1024 * 1024),
        name="tiles",
    )(cu, q, g, st, k, v)


def reduce_kernel(
    dq_ref, dk_ref, dv_ref, all_out, k_own, k_side, k_send, k_in, v_own, ring_send, ring_in, last_send, last_in,
    q_own, q_pair, q_send, q_in, send_q, recv_q, send_b, recv_b, own_sem
):
    me = Place()
    x, y, core = me.x, me.y, me.core
    sibling = me.at(flip=1)
    own = load(
        [(dv_ref, v_own), (dk_ref.at[x], k_own), (dq_ref.at[core], q_own)],
        own_sem,
    )
    greet(
        [me.at(dx=d) for d in (1, 2, 3)]
        + [me.at(dy=d) for d in (1, 2, 3)]
        + [me.at(dz=d) for d in range(1, 8)]
        + [sibling]
    )
    net = Sender(send_b, recv_b)
    rows = Sender(send_q, recv_q)
    halves = (slice(0, 2), slice(2, 4))
    parts = (slice(0, 4), slice(4, 8))
    far = me.zs(4)
    up = [[net.start(dv_ref.at[halves[0], far], ring_in.at[0, 0, halves[0]], me.at(dz=1)), None]]
    down = [[None, net.start(dv_ref.at[halves[1], far], ring_in.at[1, 0, halves[1]], me.at(dz=-1))]]
    side = []
    for part in parts:
        for d in (2, 1, 3):
            side.append(net.start(dk_ref.at[me.xs(d), part], k_side.at[d - 1, part], me.at(dx=d)))
    pair = rows.start(dq_ref.at[1 - core], q_pair, sibling)
    own[0].wait()

    def v_step(step):
        up.append([None, None])
        down.append([None, None])
        for n in (1, 0) if step == 1 else (0, 1):
            half = halves[n]
            total = v_own[half, me.zs(4 - step)].astype(F32)
            if up[step - 1][n] is not None:
                up[step - 1][n].wait_recv()
                total += ring_in[0, step - 1, half].astype(F32)
            ring_send[0, step - 1, half] = total.astype(BF16)
            up[step][n] = net.start(
                ring_send.at[0, step - 1, half], ring_in.at[0, step, half], me.at(dz=1)
            )
            n = 1 - n if step == 1 else n
            half = halves[n]
            total = v_own[half, me.zs(step - 4)].astype(F32)
            if down[step - 1][n] is not None:
                down[step - 1][n].wait_recv()
                total += ring_in[1, step - 1, half].astype(F32)
            ring_send[1, step - 1, half] = total.astype(BF16)
            down[step][n] = net.start(
                ring_send.at[1, step - 1, half], ring_in.at[1, step, half], me.at(dz=-1)
            )

    def k_part(n):
        part = parts[n]
        total = k_own[part].astype(F32)
        for m in range(3):
            side[3 * n + m].wait_recv()
        for m in range(3):
            total += k_side[m, part].astype(F32)
        k_send[part] = total.astype(BF16)

    v_step(1)
    own[2].wait()
    pair.wait_recv()
    q_rows = []
    for d in (2, 1, 3):
        slot = me.ys(d)
        q_send[d - 1] = (q_own[slot].astype(F32) + q_pair[slot].astype(F32)).astype(BF16)
        q_rows.append(rows.start(q_send.at[d - 1], q_in.at[d - 1], me.at(dy=d)))
    v_step(2)
    own[1].wait()
    k_part(0)
    v_step(3)
    k_part(1)
    k_last = [
        net.start(k_send.at[me.zs(d)], k_in.at[d - 1], me.at(dz=d)) for d in (4, 3, 5, 2, 6, 1, 7)
    ]
    here = me.zs(0)
    for n, half in enumerate(halves):
        up[3][n].wait_recv()
        down[3][n].wait_recv()
        total = v_own[half, here].astype(F32)
        total += ring_in[0, 3, half].astype(F32) + ring_in[1, 3, half].astype(F32)
        last_send[half] = total.astype(BF16)
    v_last = [net.start(last_send.at[me.xs(d)], last_in.at[d - 1], me.at(dx=d)) for d in (2, 1, 3)]
    total = q_own[y].astype(F32) + q_pair[y].astype(F32)
    for copy in q_rows:
        copy.wait_recv()
    for n in range(3):
        total += q_in[n].astype(F32)
    all_out[:, 0:COLS] = total.astype(BF16)
    for copy in k_last:
        copy.wait_recv()
    total = k_send[here].astype(F32)
    for n in range(7):
        total += k_in[n].astype(F32)
    all_out[:, COLS : COLS + HEAD_DIM] = total.astype(BF16)
    for copy in v_last:
        copy.wait_recv()
    total = last_send[x].astype(F32)
    for n in range(3):
        total += last_in[n].astype(F32)
    all_out[:, COLS + HEAD_DIM : COLS + 2 * HEAD_DIM] = total.astype(BF16)
    net.finish()
    rows.finish()


def reduce(dq, dk, dv):
    block = (SUB, HEAD_DIM)
    dma = pltpu.SemaphoreType.DMA
    return pl.pallas_call(
        reduce_kernel,
        out_shape=jax.ShapeDtypeStruct((SUB, COLS + 2 * HEAD_DIM), BF16),
        in_specs=[ANY] * 3,
        out_specs=VMEM,
        scratch_shapes=[
            pltpu.VMEM((8,) + block, BF16),
            pltpu.VMEM((3, 8) + block, BF16),
            pltpu.VMEM((8,) + block, BF16),
            pltpu.VMEM((7,) + block, BF16),
            pltpu.VMEM((4, 8) + block, BF16),
            pltpu.VMEM((2, 3, 4) + block, BF16),
            pltpu.VMEM((2, 4, 4) + block, BF16),
            pltpu.VMEM((4,) + block, BF16),
            pltpu.VMEM((3,) + block, BF16),
            pltpu.VMEM((4, SUB, COLS), BF16),
            pltpu.VMEM((4, SUB, COLS), BF16),
            pltpu.VMEM((3, SUB, COLS), BF16),
            pltpu.VMEM((3, SUB, COLS), BF16),
            dma((4,)),
            dma((4,)),
            dma((30,)),
            dma((30,)),
            dma((3,)),
        ],
        compiler_params=pltpu.CompilerParams(
            collective_id=1, has_side_effects=True, vmem_limit_bytes=63 * 1024 * 1024
        ),
        name="reduce",
    )(dq, dk, dv)


def split_kernel(all_ref, dq_ref, dk_ref, dv_ref):
    dq_ref[...] = all_ref[:, 0:COLS]
    dk_ref[...] = all_ref[:, COLS : COLS + HEAD_DIM]
    dv_ref[...] = all_ref[:, COLS + HEAD_DIM : COLS + 2 * HEAD_DIM]


def split(grads):
    return pl.pallas_call(
        split_kernel,
        out_shape=[
            jax.ShapeDtypeStruct((SUB, COLS), BF16),
            jax.ShapeDtypeStruct((SUB, HEAD_DIM), BF16),
            jax.ShapeDtypeStruct((SUB, HEAD_DIM), BF16),
        ],
        in_specs=[VMEM],
        out_specs=[VMEM] * 3,
        name="split",
    )(grads)


def per_device(query, keys, values, out, out_grad, lse, cu_seqlens, tile_table):
    q, g, k, v, st = gather(query, out_grad, keys, values, out, lse)
    shape = (16, 2 * SUB, HEAD_DIM)
    dq, dk, dv = tiles(cu_seqlens, q, g, st, k.reshape(shape), v.reshape(shape))
    blocks = (4, 8, SUB, HEAD_DIM)
    return split(reduce(dq, dk.reshape(blocks), dv.reshape(blocks)))


def solution(mesh):
    placed = (
        P(("qrow", "kcol"), None),
        P(("kcol", "qrow"), None),
        P(("kcol", "qrow"), None),
        P(("qrow", "kcol"), None),
        P(("qrow", "kcol"), None),
        P(None, ("qrow", "kcol")),
        P(),
        P("qrow", "kcol", None),
    )
    return jax.shard_map(
        per_device,
        mesh=mesh,
        in_specs=placed,
        out_specs=(P(("qrow", "kcol"), None), P(("kcol", "qrow"), None), P(("kcol", "qrow"), None)),
        check_vma=False,
    )
```

```python
import math

import jax
import jax.numpy as jnp
from jax import lax
from jax.experimental import pallas as pl
from jax.experimental.pallas import tpu as pltpu
from jax.sharding import PartitionSpec as P

MESH = pl.DeviceIdType.MESH
HEADS = 4
HEAD_DIM = 128
TILE = 512
SUB = 128
COLS = HEADS * SUB
TOKENS = 32768
SCALE = 1.0 / math.sqrt(HEAD_DIM)
LOG2E = math.log2(math.e)
LANE = (((1,), (1,)), ((), ()))
ROW = (((0,), (0,)), ((), ()))
BF16 = jnp.bfloat16
F32 = jnp.float32
VMEM = pl.BlockSpec(memory_space=pltpu.VMEM)
ANY = pl.BlockSpec(memory_space=pl.ANY)


class Place:
    def __init__(self):
        row = lax.axis_index("qrow")
        col = lax.axis_index("kcol")
        self.x = row // 4
        self.core = row % 2
        self.y = col // 4
        self.z = row // 2 % 2 * 4 + col % 4

    def at(self, dx=0, dy=0, dz=0, flip=0):
        x = (self.x + dx + 4) % 4
        y = (self.y + dy + 4) % 4
        z = (self.z + dz + 8) % 8
        core = 1 - self.core if flip else self.core
        return (x * 4 + z // 4 * 2 + core, y * 4 + z % 4)

    def xs(self, dx):
        return (self.x + dx + 4) % 4

    def ys(self, dy):
        return (self.y + dy + 4) % 4

    def zs(self, dz):
        z = (self.z + dz + 8) % 8
        return z % 4 * 2 + z // 4


class Sender:
    def __init__(self, send_sem, recv_sem):
        self.send_sem = send_sem
        self.recv_sem = recv_sem
        self.sent = []

    def start(self, src, dst, device):
        number = len(self.sent)
        copy = pltpu.make_async_remote_copy(
            src_ref=src,
            dst_ref=dst,
            send_sem=self.send_sem.at[number],
            recv_sem=self.recv_sem.at[number],
            device_id=device,
            device_id_type=MESH,
        )
        copy.start()
        self.sent.append(copy)
        return copy

    def finish(self):
        for copy in self.sent:
            copy.wait_send()


def greet(devices):
    barrier = pltpu.get_barrier_semaphore()
    for device in devices:
        pl.semaphore_signal(barrier, inc=1, device_id=device, device_id_type=MESH)
    pl.semaphore_wait(barrier, len(devices))


def load(pairs, sems):
    copies = [pltpu.make_async_copy(src, dst, sems.at[n]) for n, (src, dst) in enumerate(pairs)]
    for copy in copies:
        copy.start()
    return copies


def doc_bounds(cu_ref):
    lane = lax.broadcasted_iota(jnp.int32, (1, SUB), 1)
    low = jnp.zeros((1, SUB), jnp.int32) + TOKENS
    high = jnp.zeros((1, SUB), jnp.int32)
    for n in range(6):
        low = jnp.where(lane == 16 + n, cu_ref[n], low)
        high = jnp.where(lane == 16 + n, cu_ref[n + 1], high)
    return lane, low, high


def pieces(vec):
    out = []
    for n in range(3):
        piece = vec.astype(BF16)
        vec = vec - piece.astype(F32)
        out.append(piece)
    return out


def spot(dz):
    if abs(dz) == 4:
        return 7
    return 0 if dz == 0 else 2 * abs(dz) - (1 if dz > 0 else 0)


class Batch:
    def __init__(self, send_sem, recv_sem):
        self.send_sem = send_sem
        self.recv_sem = recv_sem

    def copy(self, src, dst, device):
        return pltpu.make_async_remote_copy(
            src_ref=src,
            dst_ref=dst,
            send_sem=self.send_sem,
            recv_sem=self.recv_sem,
            device_id=device,
            device_id_type=MESH,
        )

    def start(self, src, dst, device):
        self.copy(src, dst, device).start()


class Lane(Sender):
    def __init__(self, send_sem, recv_sem):
        super().__init__(send_sem, recv_sem)

    def start(self, src, dst, device):
        copy = pltpu.make_async_remote_copy(
            src_ref=src,
            dst_ref=dst,
            send_sem=self.send_sem,
            recv_sem=self.recv_sem.at[len(self.sent)],
            device_id=device,
            device_id_type=MESH,
        )
        copy.start()
        self.sent.append(copy)
        return copy

    def finish(self, whole, device):
        pltpu.make_async_remote_copy(
            src_ref=whole,
            dst_ref=whole,
            send_sem=self.send_sem,
            recv_sem=self.recv_sem.at[0],
            device_id=device,
            device_id_type=MESH,
        ).wait_send()


def grads_kernel(
    cu_ref, q_ref, g_ref, k_ref, v_ref, o_ref, lse_ref, all_out, ka, va, rows_in, mine, qs, gs, o_in, lse_in, feats, acc, dqa,
    stage, side_in, z_send, z_in, kept, dq_low, q_pair, q_send, q_in,
    recv_q, recv_m, recv_v, recv_k, send_x, recv_x, send_k, recv_kx, send_all, own_sem, send_s, recv_s, send_z, recv_z, send_d, recv_d
):
    me = Place()
    x, y, z, core = me.x, me.y, me.z, me.core
    here = me.zs(0)
    sibling = me.at(flip=1)
    own = load(
        [
            (k_ref, ka.at[x, here]),
            (v_ref, va.at[x, 0]),
            (q_ref, mine.at[0:SUB]),
            (g_ref, mine.at[SUB : 2 * SUB]),
            (o_ref, o_in),
            (lse_ref, lse_in),
        ],
        own_sem,
    )
    greet(
        [me.at(dx=d) for d in (1, 2, 3)]
        + [me.at(dy=d) for d in (1, 2, 3)]
        + [me.at(dz=d) for d in range(1, 8)]
        + [sibling]
    )
    rows = Lane(send_all.at[0], recv_q)
    pair = Lane(send_all.at[1], recv_m)
    v_ring = Lane(send_all.at[2], recv_v)
    k_ring = Lane(send_all.at[3], recv_k)
    k_cross = Sender(send_k, recv_kx)
    cross = {(d, n): Batch(send_x.at[d - 1, n], recv_x.at[d - 1, n]) for d in (1, 2, 3) for n in range(5)}
    k_side = [k_cross.start(k_ref, ka.at[x, here], me.at(dx=d)) for d in (2, 1, 3)]
    up = v_ring.start(v_ref, va.at[x, spot(-1)], me.at(dz=1))
    down = v_ring.start(v_ref, va.at[x, spot(1)], me.at(dz=-1))
    for d in (2, 1, 3):
        cross[d, 0].start(v_ref, va.at[x, 0], me.at(dx=d))

    def spread(first, last):
        block = va.at[x, first:last]
        for d in (2, 1, 3):
            cross[d, (first + 1) // 2].start(block, block, me.at(dx=d))

    halves = (slice(0, 2), slice(2, 4))
    k_up = []
    k_down = []

    def k_first():
        own[0].wait()
        for copy in k_side:
            copy.wait_recv()
        for half in halves:
            block = ka.at[half, here]
            k_up.append(k_ring.start(block, block, me.at(dz=1)))
            k_down.append(k_ring.start(block, block, me.at(dz=-1)))

    def k_step(step):
        for n, half in enumerate(halves):
            if step < 4 or n == 0:
                k_up[n].wait_recv()
            if step < 3 or (step == 3 and n == 0):
                block = ka.at[half, me.zs(-step)]
                k_up[n] = k_ring.start(block, block, me.at(dz=1))
            if step < 4 or n == 1:
                k_down[n].wait_recv()
            if step < 3 or (step == 3 and n == 1):
                block = ka.at[half, me.zs(step)]
                k_down[n] = k_ring.start(block, block, me.at(dz=-1))

    def v_step(up, down, step):
        up.wait_recv()
        down.wait_recv()
        if step < 3:
            up = v_ring.start(va.at[x, spot(-step)], va.at[x, spot(-step - 1)], me.at(dz=1))
            down = v_ring.start(va.at[x, spot(step)], va.at[x, spot(step + 1)], me.at(dz=-1))
        elif step == 3:
            low, high = slice(0, 64), slice(64, SUB)
            up = v_ring.start(va.at[x, spot(-3), low], va.at[x, spot(4), low], me.at(dz=1))
            down = v_ring.start(va.at[x, spot(3), high], va.at[x, spot(4), high], me.at(dz=-1))
        if step < 4:
            spread(2 * step - 1, 2 * step + 1)
        else:
            spread(7, 8)
        return up, down

    def make_rows():
        for copy in own[2:]:
            copy.wait()
        deltas = []
        for h in range(HEADS):
            lanes = slice(h * SUB, (h + 1) * SUB)
            product = o_in[:, lanes].astype(F32) * mine[SUB : 2 * SUB, lanes].astype(F32)
            deltas.append(jnp.sum(product.T, axis=0, keepdims=True))
        zero = jnp.zeros((2, SUB), BF16)
        for h in range(HEADS):
            lse_parts = pieces(lse_in[h : h + 1, :] * (-1.0 / SCALE))
            delta_parts = pieces(-deltas[h])
            mine[2 * SUB : 2 * SUB + 16, h * SUB : (h + 1) * SUB] = jnp.concatenate(
                lse_parts + delta_parts + [zero] * 5, axis=0
            )

    q_rows = {}
    q_far = []
    mirrored = {}

    def send_rows():
        mirrored[0] = pair.start(mine, rows_in.at[core, y], sibling)
        for d in (1, 3):
            q_rows[d] = rows.start(mine, rows_in.at[core, y], me.at(dy=d))

    def relay():
        q_rows[1].wait_recv()
        block = rows_in.at[core, me.ys(-1), 0:SUB]
        q_far.append(rows.start(block, block, me.at(dy=1)))
        q_rows[3].wait_recv()
        block = rows_in.at[core, me.ys(1), SUB : 2 * SUB + 16]
        q_far.append(rows.start(block, block, me.at(dy=-1)))

    def mirror(d):
        if d == 2:
            for copy in q_far:
                copy.wait_recv()
        block = rows_in.at[core, me.ys(-d)]
        mirrored[d] = pair.start(block, block, sibling)

    lane, low_cu, high_cu = doc_bounds(cu_ref)
    sub = lax.broadcasted_iota(jnp.int32, (SUB, 1), 0)

    def stack(d):
        mirrored[d].wait_recv()
        a = me.ys(-d)
        for c in range(2):
            row = x * 4 + z // 4 * 2 + c
            qpos = (a * 16 + row) * TILE + z % 4 * SUB + sub
            inside = (qpos >= low_cu) & (qpos < high_cu)
            doc_feat = jnp.where(inside | (lane < 16) | (lane >= 22), 0.0, -16384.0)
            for h in range(HEADS):
                lanes = slice(h * SUB, (h + 1) * SUB)
                to = slice(c * COLS + h * SUB, c * COLS + (h + 1) * SUB)
                qs[a, to, 0:128] = rows_in[c, a, 0:SUB, lanes]
                gs[a, to, 0:128] = rows_in[c, a, SUB : 2 * SUB, lanes]
                stat = rows_in[c, a, 2 * SUB : 2 * SUB + 16, lanes].astype(F32)
                stat = jnp.concatenate([stat, jnp.zeros((SUB - 16, SUB), F32)], axis=0).T
                lse_feat = jnp.where(lane < 3, stat, 0.0)
                delta_feat = jnp.where((lane >= 3) & (lane < 6), stat, 0.0)
                qs[a, to, 128:256] = (lse_feat + doc_feat).astype(BF16)
                gs[a, to, 128:256] = delta_feat.astype(BF16)

    i0 = x * 4 + z // 4 * 2
    zl = z % 4
    ones = lane < 6

    def key_base(b, jj):
        return (b * 16 + 4 * y + jj) * TILE + core * SUB

    def make_feats(kt, carry):
        for zh in range(2):
            pos = key_base(kt // 4, kt % 4) + zh * 2 * SUB + sub
            feats[kt, zh * SUB : (zh + 1) * SUB, :] = (
                (((pos >= low_cu) & (pos < high_cu)) | ones).astype(F32).astype(BF16)
            )
        return carry

    make_rows()
    send_rows()
    k_first()
    lax.fori_loop(0, 16, make_feats, 0)
    dqa[...] = jnp.zeros_like(dqa)
    up, down = v_step(up, down, 1)
    k_step(1)
    up, down = v_step(up, down, 2)
    stack_own = pltpu.make_async_copy(mine, rows_in.at[core, y], own_sem.at[6])
    stack_own.start()
    k_step(2)
    relay()
    mirror(1)
    mirror(3)
    up, down = v_step(up, down, 3)
    stack_own.wait()
    stack(0)
    v_step(up, down, 4)
    k_step(3)
    stack(1)
    stack(3)
    mirror(2)
    stack(2)
    own[1].wait()

    def cross_wait(n, first, last):
        for d in (1, 3, 2):
            whole = cross[d, n].copy(va.at[x, first:last], va.at[me.xs(-d), first:last], me.at(dx=d))
            whole.wait_recv()

    def tile_step(t, carry):
        g = t // 4
        n = (2 + g) % 4
        dx = (t + 1) % 4
        b = (x + dx) % 4
        jj = (zl + n) % 4
        kt = b * 4 + jj

        @pl.when(t == 0)
        def _():
            cross_wait(2, 3, 5)

        @pl.when(t == 4)
        def _():
            cross_wait(1, 1, 3)
            cross_wait(3, 5, 7)
            k_step(4)
            cross_wait(0, 0, 1)
            cross_wait(4, 7, 8)

        near = 2 * n - 1 + (3 - n) // 3
        far = 8 - 2 * n - n // 4
        far = far - (3 - n) // 3
        swap = (z + n) % 8 // 4
        v_first = near + (far - near) * swap
        v_second = far + (near - far) * swap
        keys = ka[b, pl.ds(2 * jj, 2)].reshape(2 * SUB, HEAD_DIM)
        vals = jnp.concatenate([va[b, v_first], va[b, v_second]], axis=0)
        own_tile = t % 4 // 3
        slot = 4 + (g - 4) * own_tile
        r = 4 * y + jj - i0
        acc[slot] = jnp.zeros((2, 2 * SUB, HEAD_DIM), F32)

        def unit(a, count, masked):
            wide = count * 2 * COLS
            many = pl.ds(a, count)
            feat = feats[kt]
            scores = lax.dot_general(
                jnp.concatenate([keys, feat], axis=1),
                qs[many].reshape(wide, 2 * HEAD_DIM),
                LANE,
                preferred_element_type=F32,
            )
            weights = jnp.exp2(scores * (SCALE * LOG2E))
            if masked:
                first = (a * 16 + i0) * TILE + zl * SUB
                kpos = lax.broadcasted_iota(jnp.int32, (2 * SUB, SUB), 0)
                kpos = jnp.where(kpos >= SUB, kpos + SUB, kpos) + key_base(b, jj)
                keep = [kpos <= first + lane, kpos <= first + TILE + lane]
                weights = jnp.concatenate(
                    [
                        jnp.where(keep[m // HEADS], weights[:, m * SUB : (m + 1) * SUB], 0.0)
                        for m in range(2 * HEADS)
                    ],
                    axis=1,
                )
            probs = lax.dot_general(
                jnp.concatenate([vals, feat], axis=1),
                gs[many].reshape(wide, 2 * HEAD_DIM),
                LANE,
                preferred_element_type=F32,
            )
            dscores = (weights * probs).astype(BF16)
            weights = weights.astype(BF16)
            g_rows = gs[many, :, 0:HEAD_DIM].reshape(wide, HEAD_DIM)
            q_all = qs[many, :, 0:HEAD_DIM].reshape(wide, HEAD_DIM)
            acc[slot, 0] += jnp.dot(dscores, q_all, preferred_element_type=F32)
            acc[slot, 1] += jnp.dot(weights, g_rows, preferred_element_type=F32)
            for m in range(count):
                dqa[a + m] += lax.dot_general(
                    keys,
                    dscores[:, m * 2 * COLS : (m + 1) * 2 * COLS],
                    ROW,
                    preferred_element_type=F32,
                )

        ahead = (r >= 0).astype(jnp.int32)
        start = b + ahead

        @pl.when(start <= 2)
        def _():
            unit(start, 2, False)

        @pl.when((start == 3) | ((r >= 0) & (r <= 1)))
        def _():
            single = jnp.where(start == 3, 3, b)
            unit(single, 1, True)

        @pl.when((start == 3) & (r >= 0) & (r <= 1))
        def _():
            unit(b, 1, True)

        @pl.when(own_tile == 0)
        def _():
            for zh in range(2):
                part = slice(zh * SUB, (zh + 1) * SUB)
                stage[t, zh, 0] = (acc[4, 0, part] * SCALE).astype(BF16)
                stage[t, zh, 1] = acc[4, 1, part].astype(BF16)
            side_copy(t, dx).start()

        @pl.when((t > 4) & (t % 4 == 1))
        def _():
            z_start(g - 1)

        return carry

    def side_copy(t, dx):
        return pltpu.make_async_remote_copy(
            src_ref=stage.at[t],
            dst_ref=side_in.at[t],
            send_sem=send_s.at[t],
            recv_sem=recv_s.at[t],
            device_id=me.at(dx=dx),
            device_id_type=MESH,
        )

    def z_copy(g, dz):
        return pltpu.make_async_remote_copy(
            src_ref=z_send.at[g, (z + dz) % 8 // 4],
            dst_ref=z_in.at[dz],
            send_sem=send_z.at[dz],
            recv_sem=recv_z.at[dz],
            device_id=me.at(dz=dz),
            device_id_type=MESH,
        )

    def z_start(g):
        n = (2 + g) % 4
        for e in range(3):
            side_copy(4 * g + e, e + 1).wait_recv()
        for zh in range(2):
            part = slice(zh * SUB, (zh + 1) * SUB)
            for kv in range(2):
                total = acc[g, kv, part] * (SCALE if kv == 0 else 1.0)
                for e in range(3):
                    total += side_in[4 * g + e, zh, kv].astype(F32)
                z_send[g, zh, kv] = total.astype(BF16)

        @pl.when(n > 0)
        def _():
            z_copy(g, n).start()

        z_copy(g, n + 4).start()

    lax.fori_loop(0, 16, tile_step, 0)

    for c in range(2):
        for a in range(4):
            for h in range(HEADS):
                lanes = slice(h * SUB, (h + 1) * SUB)
                to = slice(c * COLS + h * SUB, c * COLS + (h + 1) * SUB)
                dq_low[c, a, :, lanes] = (dqa[a, :, to].T * SCALE).astype(BF16)
    last = Sender(send_d, recv_d)
    swap_copy = last.start(dq_low.at[1 - core], q_pair, sibling)
    z_start(3)
    swap_copy.wait_recv()
    q_back = []
    for d in (2, 1, 3):
        a = me.ys(d)
        q_send[d - 1] = (dq_low[core, a].astype(F32) + q_pair[a].astype(F32)).astype(BF16)
        q_back.append(last.start(q_send.at[d - 1], q_in.at[d - 1], me.at(dy=d)))
    for dz in (2, 6, 3, 7, 4, 1, 5):
        z_copy((dz + 2) % 4, dz).wait_recv()
    for kv in range(2):
        total = z_send[2, z // 4, kv].astype(F32)
        for dz in range(1, 8):
            total += z_in[dz, kv].astype(F32)
        lanes = slice(COLS + kv * HEAD_DIM, COLS + (kv + 1) * HEAD_DIM)
        all_out[:, lanes] = total.astype(BF16)
    total = dq_low[core, y].astype(F32) + q_pair[y].astype(F32)
    for copy in q_back:
        copy.wait_recv()
    for m in range(3):
        total += q_in[m].astype(F32)
    all_out[:, 0:COLS] = total.astype(BF16)

    rows.finish(rows_in.at[0, 0:3], sibling)
    pair.finish(rows_in.at[0], sibling)
    v_ring.finish(va.at[x, 0:7], sibling)
    k_ring.finish(ka.at[0:4, 0:7], sibling)
    k_cross.finish()
    for n, first, size in ((0, 0, 1), (1, 1, 2), (2, 3, 2), (3, 5, 2), (4, 7, 1)):
        for d in (1, 2, 3):
            block = va.at[x, first : first + size]
            cross[d, n].copy(block, block, me.at(dx=d)).wait_send()
    for g in range(4):
        for e in range(3):
            side_copy(4 * g + e, e + 1).wait_send()
    for dz in range(1, 8):
        z_copy((dz + 2) % 4, dz).wait_send()
    last.finish()


def grads(cu, q, g, k, v, o, lse):
    dma = pltpu.SemaphoreType.DMA
    block = (SUB, HEAD_DIM)
    message = (2 * SUB + 16, COLS)
    vmem = pltpu.VMEM
    return pl.pallas_call(
        grads_kernel,
        out_shape=jax.ShapeDtypeStruct((SUB, COLS + 2 * HEAD_DIM), BF16),
        in_specs=[pl.BlockSpec(memory_space=pltpu.SMEM)] + [ANY] * 6,
        out_specs=VMEM,
        scratch_shapes=[
            vmem((4, 8) + block, BF16),
            vmem((4, 8) + block, BF16),
            vmem((2, 4) + message, BF16),
            vmem(message, BF16),
            vmem((4, 2 * COLS, 2 * HEAD_DIM), BF16),
            vmem((4, 2 * COLS, 2 * HEAD_DIM), BF16),
            vmem((SUB, COLS), BF16),
            vmem((HEADS, SUB), F32),
            vmem((16, 2 * SUB, HEAD_DIM), BF16),
            vmem((5, 2, 2 * SUB, HEAD_DIM), F32),
            vmem((4, HEAD_DIM, 2 * COLS), F32),
            vmem((16, 2, 2) + block, BF16),
            vmem((16, 2, 2) + block, BF16),
            vmem((4, 2, 2) + block, BF16),
            vmem((8, 2) + block, BF16),
            vmem((8, 128), F32),
            vmem((2, 4, SUB, COLS), BF16),
            vmem((4, SUB, COLS), BF16),
            vmem((3, SUB, COLS), BF16),
            vmem((3, SUB, COLS), BF16),
            dma((4,)),
            dma((4,)),
            dma((8,)),
            dma((14,)),
            dma((3, 5)),
            dma((3, 5)),
            dma((3,)),
            dma((3,)),
            dma((4,)),
            dma((7,)),
            dma((16,)),
            dma((16,)),
            dma((8,)),
            dma((8,)),
            dma((4,)),
            dma((4,)),
        ],
        compiler_params=pltpu.CompilerParams(
            collective_id=0, has_side_effects=True, vmem_limit_bytes=63 * 1024 * 1024
        ),
        name="grads",
    )(cu, q, g, k, v, o, lse)


def split_kernel(all_ref, dq_ref, dk_ref, dv_ref):
    dq_ref[...] = all_ref[:, 0:COLS]
    dk_ref[...] = all_ref[:, COLS : COLS + HEAD_DIM]
    dv_ref[...] = all_ref[:, COLS + HEAD_DIM : COLS + 2 * HEAD_DIM]


def split(grads):
    return pl.pallas_call(
        split_kernel,
        out_shape=[
            jax.ShapeDtypeStruct((SUB, COLS), BF16),
            jax.ShapeDtypeStruct((SUB, HEAD_DIM), BF16),
            jax.ShapeDtypeStruct((SUB, HEAD_DIM), BF16),
        ],
        in_specs=[VMEM],
        out_specs=[VMEM] * 3,
        name="split",
    )(grads)


def per_device(query, keys, values, out, out_grad, lse, cu_seqlens, tile_table):
    return split(grads(cu_seqlens, query, out_grad, keys, values, out, lse))


def solution(mesh):
    placed = (
        P(("qrow", "kcol"), None),
        P(("kcol", "qrow"), None),
        P(("kcol", "qrow"), None),
        P(("qrow", "kcol"), None),
        P(("qrow", "kcol"), None),
        P(None, ("qrow", "kcol")),
        P(),
        P("qrow", "kcol", None),
    )
    return jax.shard_map(
        per_device,
        mesh=mesh,
        in_specs=placed,
        out_specs=(P(("qrow", "kcol"), None), P(("kcol", "qrow"), None), P(("kcol", "qrow"), None)),
        check_vma=False,
    )
```

```python
import math

import jax
import jax.numpy as jnp
from jax import lax
from jax.experimental import pallas as pl
from jax.experimental.pallas import tpu as pltpu
from jax.sharding import PartitionSpec as P

MESH = pl.DeviceIdType.MESH
HEADS = 4
HEAD_DIM = 128
TILE = 512
SUB = 128
COLS = HEADS * SUB
TOKENS = 32768
SCALE = 1.0 / math.sqrt(HEAD_DIM)
LOG2E = math.log2(math.e)
LANE = (((1,), (1,)), ((), ()))
ROW = (((0,), (0,)), ((), ()))
BF16 = jnp.bfloat16
F32 = jnp.float32
VMEM = pl.BlockSpec(memory_space=pltpu.VMEM)
ANY = pl.BlockSpec(memory_space=pl.ANY)


class Place:
    def __init__(self):
        row = lax.axis_index("qrow")
        col = lax.axis_index("kcol")
        self.x = row // 4
        self.core = row % 2
        self.y = col // 4
        self.z = row // 2 % 2 * 4 + col % 4

    def at(self, dx=0, dy=0, dz=0, flip=0):
        x = (self.x + dx + 4) % 4
        y = (self.y + dy + 4) % 4
        z = (self.z + dz + 8) % 8
        core = 1 - self.core if flip else self.core
        return (x * 4 + z // 4 * 2 + core, y * 4 + z % 4)

    def xs(self, dx):
        return (self.x + dx + 4) % 4

    def ys(self, dy):
        return (self.y + dy + 4) % 4

    def zs(self, dz):
        z = (self.z + dz + 8) % 8
        return z % 4 * 2 + z // 4


class Sender:
    def __init__(self, send_sem, recv_sem):
        self.send_sem = send_sem
        self.recv_sem = recv_sem
        self.sent = []

    def start(self, src, dst, device):
        number = len(self.sent)
        copy = pltpu.make_async_remote_copy(
            src_ref=src,
            dst_ref=dst,
            send_sem=self.send_sem.at[number],
            recv_sem=self.recv_sem.at[number],
            device_id=device,
            device_id_type=MESH,
        )
        copy.start()
        self.sent.append(copy)
        return copy

    def finish(self):
        for copy in self.sent:
            copy.wait_send()


def greet(devices):
    barrier = pltpu.get_barrier_semaphore()
    for device in devices:
        pl.semaphore_signal(barrier, inc=1, device_id=device, device_id_type=MESH)
    pl.semaphore_wait(barrier, len(devices))


def load(pairs, sems):
    copies = [pltpu.make_async_copy(src, dst, sems.at[n]) for n, (src, dst) in enumerate(pairs)]
    for copy in copies:
        copy.start()
    return copies


def doc_bounds(cu_ref):
    lane = lax.broadcasted_iota(jnp.int32, (1, SUB), 1)
    low = jnp.zeros((1, SUB), jnp.int32) + TOKENS
    high = jnp.zeros((1, SUB), jnp.int32)
    for n in range(6):
        low = jnp.where(lane == 16 + n, cu_ref[n], low)
        high = jnp.where(lane == 16 + n, cu_ref[n + 1], high)
    return lane, low, high


def pieces(vec):
    out = []
    for n in range(3):
        piece = vec.astype(BF16)
        vec = vec - piece.astype(F32)
        out.append(piece)
    return out


def spot(dz):
    if abs(dz) == 4:
        return 7
    return 0 if dz == 0 else 2 * abs(dz) - (1 if dz > 0 else 0)


class Batch:
    def __init__(self, send_sem, recv_sem):
        self.send_sem = send_sem
        self.recv_sem = recv_sem

    def copy(self, src, dst, device):
        return pltpu.make_async_remote_copy(
            src_ref=src,
            dst_ref=dst,
            send_sem=self.send_sem,
            recv_sem=self.recv_sem,
            device_id=device,
            device_id_type=MESH,
        )

    def start(self, src, dst, device):
        self.copy(src, dst, device).start()


class Lane(Sender):
    def __init__(self, send_sem, recv_sem):
        super().__init__(send_sem, recv_sem)

    def start(self, src, dst, device):
        copy = pltpu.make_async_remote_copy(
            src_ref=src,
            dst_ref=dst,
            send_sem=self.send_sem,
            recv_sem=self.recv_sem.at[len(self.sent)],
            device_id=device,
            device_id_type=MESH,
        )
        copy.start()
        self.sent.append(copy)
        return copy

    def finish(self, whole, device):
        pltpu.make_async_remote_copy(
            src_ref=whole,
            dst_ref=whole,
            send_sem=self.send_sem,
            recv_sem=self.recv_sem.at[0],
            device_id=device,
            device_id_type=MESH,
        ).wait_send()


def grads_kernel(
    cu_ref, q_ref, g_ref, k_ref, v_ref, o_ref, lse_ref, all_out, ka, va, rows_in, mine, qs, gs, o_in, lse_in, feats, acc, dqa,
    stage, side_in, z_send, z_in, dq_low, q_pair, q_send, q_in,
    recv_q, recv_m, recv_v, recv_k, send_x, recv_x, send_k, recv_kx, send_all, own_sem, send_s, recv_s, send_z, recv_z, send_d, recv_d
):
    me = Place()
    x, y, z, core = me.x, me.y, me.z, me.core
    here = me.zs(0)
    sibling = me.at(flip=1)
    own = load(
        [
            (k_ref, ka.at[x, here]),
            (v_ref, va.at[x, 0]),
            (q_ref, mine.at[0:SUB]),
            (g_ref, mine.at[SUB : 2 * SUB]),
            (o_ref, o_in),
            (lse_ref, lse_in),
        ],
        own_sem,
    )
    greet(
        [me.at(dx=d) for d in (1, 2, 3)]
        + [me.at(dy=d) for d in (1, 2, 3)]
        + [me.at(dz=d) for d in range(1, 8)]
        + [sibling]
    )
    rows = Lane(send_all.at[0], recv_q)
    pair = Lane(send_all.at[1], recv_m)
    v_ring = Lane(send_all.at[2], recv_v)
    k_ring = Lane(send_all.at[3], recv_k)
    k_cross = Sender(send_k, recv_kx)
    cross = {(d, n): Batch(send_x.at[d - 1, n], recv_x.at[d - 1, n]) for d in (1, 2, 3) for n in range(5)}
    k_side = [k_cross.start(k_ref, ka.at[x, here], me.at(dx=d)) for d in (2, 1, 3)]
    v_in = {d: v_ring.start(v_ref, va.at[x, spot(-d)], me.at(dz=d)) for d in (1, -1, 2, -2, 3, -3, 4)}
    for d in (2, 1, 3):
        cross[d, 0].start(v_ref, va.at[x, 0], me.at(dx=d))

    def spread(first, last):
        block = va.at[x, first:last]
        for d in (2, 1, 3):
            cross[d, (first + 1) // 2].start(block, block, me.at(dx=d))

    halves = (slice(0, 2), slice(2, 4))
    k_up = []
    k_down = []

    def k_first():
        own[0].wait()
        for copy in k_side:
            copy.wait_recv()
        for half in halves:
            block = ka.at[half, here]
            k_up.append(k_ring.start(block, block, me.at(dz=1)))
            k_down.append(k_ring.start(block, block, me.at(dz=-1)))

    def k_step(step):
        for n, half in enumerate(halves):
            if step < 4 or n == 0:
                k_up[n].wait_recv()
            if step < 3 or (step == 3 and n == 0):
                block = ka.at[half, me.zs(-step)]
                k_up[n] = k_ring.start(block, block, me.at(dz=1))
            if step < 4 or n == 1:
                k_down[n].wait_recv()
            if step < 3 or (step == 3 and n == 1):
                block = ka.at[half, me.zs(step)]
                k_down[n] = k_ring.start(block, block, me.at(dz=-1))

    def v_step(step):
        v_in[step].wait_recv()
        if step < 4:
            v_in[-step].wait_recv()
            spread(2 * step - 1, 2 * step + 1)
        else:
            spread(7, 8)

    def make_rows():
        for copy in own[2:]:
            copy.wait()
        deltas = []
        for h in range(HEADS):
            lanes = slice(h * SUB, (h + 1) * SUB)
            product = o_in[:, lanes].astype(F32) * mine[SUB : 2 * SUB, lanes].astype(F32)
            deltas.append(jnp.sum(product.T, axis=0, keepdims=True))
        zero = jnp.zeros((2, SUB), BF16)
        for h in range(HEADS):
            lse_parts = pieces(lse_in[h : h + 1, :] * (-1.0 / SCALE))
            delta_parts = pieces(-deltas[h])
            mine[2 * SUB : 2 * SUB + 16, h * SUB : (h + 1) * SUB] = jnp.concatenate(
                lse_parts + delta_parts + [zero] * 5, axis=0
            )

    q_rows = {}
    q_far = []
    mirrored = {}

    def send_rows():
        mirrored[0] = pair.start(mine, rows_in.at[core, y], sibling)
        for d in (1, 3):
            q_rows[d] = rows.start(mine, rows_in.at[core, y], me.at(dy=d))

    def relay():
        q_rows[1].wait_recv()
        block = rows_in.at[core, me.ys(-1), 0:SUB]
        q_far.append(rows.start(block, block, me.at(dy=1)))
        q_rows[3].wait_recv()
        block = rows_in.at[core, me.ys(1), SUB : 2 * SUB + 16]
        q_far.append(rows.start(block, block, me.at(dy=-1)))

    def mirror(d):
        if d == 2:
            for copy in q_far:
                copy.wait_recv()
        block = rows_in.at[core, me.ys(-d)]
        mirrored[d] = pair.start(block, block, sibling)

    lane, low_cu, high_cu = doc_bounds(cu_ref)
    sub = lax.broadcasted_iota(jnp.int32, (SUB, 1), 0)

    def stack(d):
        mirrored[d].wait_recv()
        a = me.ys(-d)
        for c in range(2):
            row = x * 4 + z // 4 * 2 + c
            qpos = (a * 16 + row) * TILE + z % 4 * SUB + sub
            inside = (qpos >= low_cu) & (qpos < high_cu)
            doc_feat = jnp.where(inside | (lane < 16) | (lane >= 22), 0.0, -16384.0)
            for h in range(HEADS):
                lanes = slice(h * SUB, (h + 1) * SUB)
                to = slice(c * COLS + h * SUB, c * COLS + (h + 1) * SUB)
                qs[a, to, 0:128] = rows_in[c, a, 0:SUB, lanes]
                gs[a, to, 0:128] = rows_in[c, a, SUB : 2 * SUB, lanes]
                stat = rows_in[c, a, 2 * SUB : 2 * SUB + 16, lanes].astype(F32)
                stat = jnp.concatenate([stat, jnp.zeros((SUB - 16, SUB), F32)], axis=0).T
                lse_feat = jnp.where(lane < 3, stat, 0.0)
                delta_feat = jnp.where((lane >= 3) & (lane < 6), stat, 0.0)
                qs[a, to, 128:256] = (lse_feat + doc_feat).astype(BF16)
                gs[a, to, 128:256] = delta_feat.astype(BF16)

    i0 = x * 4 + z // 4 * 2
    zl = z % 4
    ones = lane < 6

    def key_base(b, jj):
        return (b * 16 + 4 * y + jj) * TILE + core * SUB

    def make_feats(kt, carry):
        for zh in range(2):
            pos = key_base(kt // 4, kt % 4) + zh * 2 * SUB + sub
            feats[kt, zh * SUB : (zh + 1) * SUB, :] = (
                (((pos >= low_cu) & (pos < high_cu)) | ones).astype(F32).astype(BF16)
            )
        return carry

    make_rows()
    send_rows()
    stack_own = pltpu.make_async_copy(mine, rows_in.at[core, y], own_sem.at[6])
    stack_own.start()
    k_first()
    v_step(1)
    lax.fori_loop(0, 16, make_feats, 0)
    dqa[...] = jnp.zeros_like(dqa)
    v_step(2)
    k_step(1)
    v_step(3)
    v_step(4)
    relay()
    mirror(1)
    mirror(3)
    stack_own.wait()
    stack(0)
    k_step(2)
    stack(1)
    stack(3)
    mirror(2)
    k_step(3)
    stack(2)
    own[1].wait()

    def cross_wait(n, first, last):
        for d in (1, 3, 2):
            whole = cross[d, n].copy(va.at[x, first:last], va.at[me.xs(-d), first:last], me.at(dx=d))
            whole.wait_recv()

    def tile_step(t, carry):
        g = t // 4
        n = (2 + g) % 4
        dx = (t + 1) % 4
        b = (x + dx) % 4
        jj = (zl + n) % 4
        kt = b * 4 + jj

        @pl.when(t == 0)
        def _():
            cross_wait(2, 3, 5)

        @pl.when(t == 4)
        def _():
            cross_wait(1, 1, 3)
            cross_wait(3, 5, 7)
            k_step(4)
            cross_wait(0, 0, 1)
            cross_wait(4, 7, 8)

        near = 2 * n - 1 + (3 - n) // 3
        far = 8 - 2 * n - n // 4
        far = far - (3 - n) // 3
        swap = (z + n) % 8 // 4
        v_first = near + (far - near) * swap
        v_second = far + (near - far) * swap
        keys = ka[b, pl.ds(2 * jj, 2)].reshape(2 * SUB, HEAD_DIM)
        vals = jnp.concatenate([va[b, v_first], va[b, v_second]], axis=0)
        own_tile = t % 4 // 3
        slot = 4 + (g - 4) * own_tile
        r = 4 * y + jj - i0
        acc[slot] = jnp.zeros((2, 2 * SUB, HEAD_DIM), F32)

        def unit(a, count, masked):
            wide = count * 2 * COLS
            many = pl.ds(a, count)
            feat = feats[kt]
            scores = lax.dot_general(
                jnp.concatenate([keys, feat], axis=1),
                qs[many].reshape(wide, 2 * HEAD_DIM),
                LANE,
                preferred_element_type=F32,
            )
            weights = jnp.exp2(scores * (SCALE * LOG2E))
            if masked:
                first = (a * 16 + i0) * TILE + zl * SUB
                kpos = lax.broadcasted_iota(jnp.int32, (2 * SUB, SUB), 0)
                kpos = jnp.where(kpos >= SUB, kpos + SUB, kpos) + key_base(b, jj)
                keep = [kpos <= first + lane, kpos <= first + TILE + lane]
                weights = jnp.concatenate(
                    [
                        jnp.where(keep[m // HEADS], weights[:, m * SUB : (m + 1) * SUB], 0.0)
                        for m in range(2 * HEADS)
                    ],
                    axis=1,
                )
            probs = lax.dot_general(
                jnp.concatenate([vals, feat], axis=1),
                gs[many].reshape(wide, 2 * HEAD_DIM),
                LANE,
                preferred_element_type=F32,
            )
            dscores = (weights * probs).astype(BF16)
            weights = weights.astype(BF16)
            g_rows = gs[many, :, 0:HEAD_DIM].reshape(wide, HEAD_DIM)
            q_all = qs[many, :, 0:HEAD_DIM].reshape(wide, HEAD_DIM)
            acc[slot, 0] += jnp.dot(dscores, q_all, preferred_element_type=F32)
            acc[slot, 1] += jnp.dot(weights, g_rows, preferred_element_type=F32)
            for m in range(count):
                dqa[a + m] += lax.dot_general(
                    keys,
                    dscores[:, m * 2 * COLS : (m + 1) * 2 * COLS],
                    ROW,
                    preferred_element_type=F32,
                )

        def half_unit(a):
            feat = feats[kt]
            q_half = qs[a, COLS : 2 * COLS]
            g_half = gs[a, COLS : 2 * COLS]
            scores = lax.dot_general(
                jnp.concatenate([keys, feat], axis=1), q_half, LANE, preferred_element_type=F32
            )
            weights = jnp.exp2(scores * (SCALE * LOG2E))
            kpos = lax.broadcasted_iota(jnp.int32, (2 * SUB, SUB), 0)
            kpos = jnp.where(kpos >= SUB, kpos + SUB, kpos)
            keep = kpos + core * SUB <= zl * SUB + lane
            weights = jnp.concatenate(
                [jnp.where(keep, weights[:, m * SUB : (m + 1) * SUB], 0.0) for m in range(HEADS)],
                axis=1,
            )
            probs = lax.dot_general(
                jnp.concatenate([vals, feat], axis=1), g_half, LANE, preferred_element_type=F32
            )
            dscores = (weights * probs).astype(BF16)
            weights = weights.astype(BF16)
            acc[slot, 0] += jnp.dot(dscores, q_half[:, 0:HEAD_DIM], preferred_element_type=F32)
            acc[slot, 1] += jnp.dot(weights, g_half[:, 0:HEAD_DIM], preferred_element_type=F32)
            dqa[a, :, COLS : 2 * COLS] += lax.dot_general(
                keys, dscores, ROW, preferred_element_type=F32
            )

        ahead = (r >= 0).astype(jnp.int32)
        start = b + ahead

        @pl.when(start <= 2)
        def _():
            unit(start, 2, False)

        def single(u, carry):
            unit(jnp.where(u == 0, 3, b), 1, True)
            return carry

        lax.fori_loop(jnp.where(start == 3, 0, 1), jnp.where(r == 0, 2, 1), single, 0)

        @pl.when(r == 1)
        def _():
            half_unit(b)

        @pl.when(own_tile == 0)
        def _():
            for zh in range(2):
                part = slice(zh * SUB, (zh + 1) * SUB)
                stage[t, zh, 0] = (acc[4, 0, part] * SCALE).astype(BF16)
                stage[t, zh, 1] = acc[4, 1, part].astype(BF16)
            side_copy(t, dx).start()

        @pl.when((t > 4) & (t % 4 == 3))
        def _():
            z_start(g - 1)

        return carry

    def side_copy(t, dx):
        return pltpu.make_async_remote_copy(
            src_ref=stage.at[t],
            dst_ref=side_in.at[t],
            send_sem=send_s.at[t],
            recv_sem=recv_s.at[t],
            device_id=me.at(dx=dx),
            device_id_type=MESH,
        )

    def z_copy(g, dz):
        return pltpu.make_async_remote_copy(
            src_ref=z_send.at[g, (z + dz) % 8 // 4],
            dst_ref=z_in.at[dz],
            send_sem=send_z.at[dz],
            recv_sem=recv_z.at[dz],
            device_id=me.at(dz=dz),
            device_id_type=MESH,
        )

    def z_start(g):
        n = (2 + g) % 4
        for e in range(3):
            side_copy(4 * g + e, e + 1).wait_recv()
        for zh in range(2):
            part = slice(zh * SUB, (zh + 1) * SUB)
            for kv in range(2):
                total = acc[g, kv, part] * (SCALE if kv == 0 else 1.0)
                for e in range(3):
                    total += side_in[4 * g + e, zh, kv].astype(F32)
                z_send[g, zh, kv] = total.astype(BF16)

        @pl.when(n > 0)
        def _():
            z_copy(g, n).start()

        z_copy(g, n + 4).start()

    lax.fori_loop(0, 16, tile_step, 0)

    last = Sender(send_d, recv_d)
    swaps = {}

    def dq_swap(d):
        a = me.ys(d)
        for c in range(2):
            for h in range(HEADS):
                lanes = slice(h * SUB, (h + 1) * SUB)
                to = slice(c * COLS + h * SUB, c * COLS + (h + 1) * SUB)
                dq_low[c, a, :, lanes] = (dqa[a, :, to].T * SCALE).astype(BF16)
        swaps[d] = last.start(dq_low.at[1 - core, a], q_pair.at[a], sibling)

    q_back = []

    def dq_send(d):
        a = me.ys(d)
        swaps[d].wait_recv()
        q_send[d - 1] = (dq_low[core, a].astype(F32) + q_pair[a].astype(F32)).astype(BF16)
        q_back.append(last.start(q_send.at[d - 1], q_in.at[d - 1], me.at(dy=d)))

    dq_swap(2)
    dq_swap(1)
    dq_swap(3)
    dq_send(2)
    dq_send(1)
    dq_send(3)
    z_start(3)
    dq_swap(0)
    swaps[0].wait_recv()
    for dz in (2, 6, 3, 7, 4, 1, 5):
        z_copy((dz + 2) % 4, dz).wait_recv()
    for kv in range(2):
        total = z_send[2, z // 4, kv].astype(F32)
        for dz in range(1, 8):
            total += z_in[dz, kv].astype(F32)
        lanes = slice(COLS + kv * HEAD_DIM, COLS + (kv + 1) * HEAD_DIM)
        all_out[:, lanes] = total.astype(BF16)
    total = dq_low[core, y].astype(F32) + q_pair[y].astype(F32)
    for copy in q_back:
        copy.wait_recv()
    for m in range(3):
        total += q_in[m].astype(F32)
    all_out[:, 0:COLS] = total.astype(BF16)

    rows.finish(rows_in.at[0, 0:3], sibling)
    pair.finish(rows_in.at[0], sibling)
    v_ring.finish(va.at[x, 0:7], sibling)
    k_ring.finish(ka.at[0:4, 0:7], sibling)
    k_cross.finish()
    for n, first, size in ((0, 0, 1), (1, 1, 2), (2, 3, 2), (3, 5, 2), (4, 7, 1)):
        for d in (1, 2, 3):
            block = va.at[x, first : first + size]
            cross[d, n].copy(block, block, me.at(dx=d)).wait_send()
    for g in range(4):
        for e in range(3):
            side_copy(4 * g + e, e + 1).wait_send()
    for dz in range(1, 8):
        z_copy((dz + 2) % 4, dz).wait_send()
    last.finish()


def grads(cu, q, g, k, v, o, lse):
    dma = pltpu.SemaphoreType.DMA
    block = (SUB, HEAD_DIM)
    message = (2 * SUB + 16, COLS)
    vmem = pltpu.VMEM
    return pl.pallas_call(
        grads_kernel,
        out_shape=jax.ShapeDtypeStruct((SUB, COLS + 2 * HEAD_DIM), BF16),
        in_specs=[pl.BlockSpec(memory_space=pltpu.SMEM)] + [ANY] * 6,
        out_specs=VMEM,
        scratch_shapes=[
            vmem((4, 8) + block, BF16),
            vmem((4, 8) + block, BF16),
            vmem((2, 4) + message, BF16),
            vmem(message, BF16),
            vmem((4, 2 * COLS, 2 * HEAD_DIM), BF16),
            vmem((4, 2 * COLS, 2 * HEAD_DIM), BF16),
            vmem((SUB, COLS), BF16),
            vmem((HEADS, SUB), F32),
            vmem((16, 2 * SUB, HEAD_DIM), BF16),
            vmem((5, 2, 2 * SUB, HEAD_DIM), F32),
            vmem((4, HEAD_DIM, 2 * COLS), F32),
            vmem((16, 2, 2) + block, BF16),
            vmem((16, 2, 2) + block, BF16),
            vmem((4, 2, 2) + block, BF16),
            vmem((8, 2) + block, BF16),
            vmem((2, 4, SUB, COLS), BF16),
            vmem((4, SUB, COLS), BF16),
            vmem((3, SUB, COLS), BF16),
            vmem((3, SUB, COLS), BF16),
            dma((4,)),
            dma((4,)),
            dma((8,)),
            dma((14,)),
            dma((3, 5)),
            dma((3, 5)),
            dma((3,)),
            dma((3,)),
            dma((4,)),
            dma((7,)),
            dma((16,)),
            dma((16,)),
            dma((8,)),
            dma((8,)),
            dma((7,)),
            dma((7,)),
        ],
        compiler_params=pltpu.CompilerParams(
            collective_id=0, has_side_effects=True, vmem_limit_bytes=63 * 1024 * 1024
        ),
        name="grads",
    )(cu, q, g, k, v, o, lse)


def split_kernel(all_ref, dq_ref, dk_ref, dv_ref):
    dq_ref[...] = all_ref[:, 0:COLS]
    dk_ref[...] = all_ref[:, COLS : COLS + HEAD_DIM]
    dv_ref[...] = all_ref[:, COLS + HEAD_DIM : COLS + 2 * HEAD_DIM]


def split(grads):
    return pl.pallas_call(
        split_kernel,
        out_shape=[
            jax.ShapeDtypeStruct((SUB, COLS), BF16),
            jax.ShapeDtypeStruct((SUB, HEAD_DIM), BF16),
            jax.ShapeDtypeStruct((SUB, HEAD_DIM), BF16),
        ],
        in_specs=[VMEM],
        out_specs=[VMEM] * 3,
        name="split",
    )(grads)


def per_device(query, keys, values, out, out_grad, lse, cu_seqlens, tile_table):
    return split(grads(cu_seqlens, query, out_grad, keys, values, out, lse))


def solution(mesh):
    placed = (
        P(("qrow", "kcol"), None),
        P(("kcol", "qrow"), None),
        P(("kcol", "qrow"), None),
        P(("qrow", "kcol"), None),
        P(("qrow", "kcol"), None),
        P(None, ("qrow", "kcol")),
        P(),
        P("qrow", "kcol", None),
    )
    return jax.shard_map(
        per_device,
        mesh=mesh,
        in_specs=placed,
        out_specs=(P(("qrow", "kcol"), None), P(("kcol", "qrow"), None), P(("kcol", "qrow"), None)),
        check_vma=False,
    )
```

```python
import math

import jax
import jax.numpy as jnp
from jax import lax
from jax.experimental import pallas as pl
from jax.experimental.pallas import tpu as pltpu
from jax.sharding import PartitionSpec as P

MESH = pl.DeviceIdType.MESH
HEADS = 4
HEAD_DIM = 128
TILE = 512
SUB = 128
COLS = HEADS * SUB
TOKENS = 32768
SCALE = 1.0 / math.sqrt(HEAD_DIM)
LOG2E = math.log2(math.e)
LANE = (((1,), (1,)), ((), ()))
ROW = (((0,), (0,)), ((), ()))
BF16 = jnp.bfloat16
F32 = jnp.float32
VMEM = pl.BlockSpec(memory_space=pltpu.VMEM)
ANY = pl.BlockSpec(memory_space=pl.ANY)


class Place:
    def __init__(self):
        row = lax.axis_index("qrow")
        col = lax.axis_index("kcol")
        self.x = row // 4
        self.core = row % 2
        self.y = col // 4
        self.z = row // 2 % 2 * 4 + col % 4

    def at(self, dx=0, dy=0, dz=0, flip=0):
        x = (self.x + dx + 4) % 4
        y = (self.y + dy + 4) % 4
        z = (self.z + dz + 8) % 8
        core = 1 - self.core if flip else self.core
        return (x * 4 + z // 4 * 2 + core, y * 4 + z % 4)

    def xs(self, dx):
        return (self.x + dx + 4) % 4

    def ys(self, dy):
        return (self.y + dy + 4) % 4

    def zs(self, dz):
        z = (self.z + dz + 8) % 8
        return z % 4 * 2 + z // 4


class Sender:
    def __init__(self, send_sem, recv_sem):
        self.send_sem = send_sem
        self.recv_sem = recv_sem
        self.sent = []

    def start(self, src, dst, device):
        number = len(self.sent)
        copy = pltpu.make_async_remote_copy(
            src_ref=src,
            dst_ref=dst,
            send_sem=self.send_sem.at[number],
            recv_sem=self.recv_sem.at[number],
            device_id=device,
            device_id_type=MESH,
        )
        copy.start()
        self.sent.append(copy)
        return copy

    def finish(self):
        for copy in self.sent:
            copy.wait_send()


def greet(devices):
    barrier = pltpu.get_barrier_semaphore()
    for device in devices:
        pl.semaphore_signal(barrier, inc=1, device_id=device, device_id_type=MESH)
    pl.semaphore_wait(barrier, len(devices))


def load(pairs, sems):
    copies = [pltpu.make_async_copy(src, dst, sems.at[n]) for n, (src, dst) in enumerate(pairs)]
    for copy in copies:
        copy.start()
    return copies


def doc_bounds(cu_ref):
    lane = lax.broadcasted_iota(jnp.int32, (1, SUB), 1)
    low = jnp.zeros((1, SUB), jnp.int32) + TOKENS
    high = jnp.zeros((1, SUB), jnp.int32)
    for n in range(6):
        low = jnp.where(lane == 16 + n, cu_ref[n], low)
        high = jnp.where(lane == 16 + n, cu_ref[n + 1], high)
    return lane, low, high


def pieces(vec):
    out = []
    for n in range(3):
        piece = vec.astype(BF16)
        vec = vec - piece.astype(F32)
        out.append(piece)
    return out


def spot(dz):
    if abs(dz) == 4:
        return 7
    return 0 if dz == 0 else 2 * abs(dz) - (1 if dz > 0 else 0)


class Batch:
    def __init__(self, send_sem, recv_sem):
        self.send_sem = send_sem
        self.recv_sem = recv_sem

    def copy(self, src, dst, device):
        return pltpu.make_async_remote_copy(
            src_ref=src,
            dst_ref=dst,
            send_sem=self.send_sem,
            recv_sem=self.recv_sem,
            device_id=device,
            device_id_type=MESH,
        )

    def start(self, src, dst, device):
        self.copy(src, dst, device).start()


class Lane(Sender):
    def __init__(self, send_sem, recv_sem):
        super().__init__(send_sem, recv_sem)

    def start(self, src, dst, device):
        copy = pltpu.make_async_remote_copy(
            src_ref=src,
            dst_ref=dst,
            send_sem=self.send_sem,
            recv_sem=self.recv_sem.at[len(self.sent)],
            device_id=device,
            device_id_type=MESH,
        )
        copy.start()
        self.sent.append(copy)
        return copy

    def finish(self, whole, device):
        pltpu.make_async_remote_copy(
            src_ref=whole,
            dst_ref=whole,
            send_sem=self.send_sem,
            recv_sem=self.recv_sem.at[0],
            device_id=device,
            device_id_type=MESH,
        ).wait_send()


def grads_kernel(
    cu_ref, q_ref, g_ref, k_ref, v_ref, o_ref, lse_ref, all_out, ka, va, rows_in, mine, qs, gs, o_in, lse_in, feats, acc, dqa,
    stage, side_in, z_send, z_in, dq_low, q_pair, q_send, q_in,
    recv_q, recv_m, recv_v, recv_k, send_x, recv_x, send_k, recv_kx, send_all, own_sem, send_s, recv_s, send_z, recv_z, send_d, recv_d
):
    me = Place()
    x, y, z, core = me.x, me.y, me.z, me.core
    here = me.zs(0)
    sibling = me.at(flip=1)
    own = load(
        [
            (k_ref, ka.at[x, here]),
            (v_ref, va.at[x, 0]),
            (q_ref, mine.at[0:SUB]),
            (g_ref, mine.at[SUB : 2 * SUB]),
            (o_ref, o_in),
            (lse_ref, lse_in),
        ],
        own_sem,
    )
    greet(
        [me.at(dx=d) for d in (1, 2, 3)]
        + [me.at(dy=d) for d in (1, 2, 3)]
        + [me.at(dz=d) for d in range(1, 8)]
        + [sibling]
    )
    rows = Lane(send_all.at[0], recv_q)
    pair = Lane(send_all.at[1], recv_m)
    v_ring = Lane(send_all.at[2], recv_v)
    k_ring = Lane(send_all.at[3], recv_k)
    k_cross = Sender(send_k, recv_kx)
    q_part, g_part, s_part = slice(0, SUB), slice(SUB, 2 * SUB), slice(2 * SUB, 2 * SUB + 16)
    mirrored = {}
    q_rows = {1: [], 2: [], 3: []}

    def send_rows():
        for n in range(2):
            for d, part, src in ((1, q_part, q_ref), (3, g_part, g_ref)) if n == 0 else (
                (1, g_part, g_ref),
                (3, q_part, q_ref),
            ):
                q_rows[d].append(rows.start(src, rows_in.at[core, y, part], me.at(dy=d)))

    cross = {(d, n): Batch(send_x.at[d - 1, n], recv_x.at[d - 1, n]) for d in (1, 2, 3) for n in range(5)}
    send_rows()
    k_side = [k_cross.start(k_ref, ka.at[x, here], me.at(dx=d)) for d in (2, 1, 3)]
    v_in = {d: v_ring.start(v_ref, va.at[x, spot(-d)], me.at(dz=d)) for d in (1, -1, 2, -2, 3, -3, 4)}
    for d in (2, 1, 3):
        cross[d, 0].start(v_ref, va.at[x, 0], me.at(dx=d))

    def spread(first, last):
        block = va.at[x, first:last]
        for d in (2, 1, 3):
            cross[d, (first + 1) // 2].start(block, block, me.at(dx=d))

    halves = (slice(0, 2), slice(2, 4))
    k_up = []
    k_down = []

    def k_first():
        own[0].wait()
        for copy in k_side:
            copy.wait_recv()
        for half in halves:
            block = ka.at[half, here]
            k_up.append(k_ring.start(block, block, me.at(dz=1)))
            k_down.append(k_ring.start(block, block, me.at(dz=-1)))

    def k_step(step):
        for n, half in enumerate(halves):
            k_up[n].wait_recv()
            block = ka.at[half, me.zs(-step)]
            k_up[n] = k_ring.start(block, block, me.at(dz=1))
            k_down[n].wait_recv()
            block = ka.at[half, me.zs(step)]
            k_down[n] = k_ring.start(block, block, me.at(dz=-1))

    def v_step(step):
        v_in[step].wait_recv()
        if step < 4:
            v_in[-step].wait_recv()
            spread(2 * step - 1, 2 * step + 1)
        else:
            spread(7, 8)

    def make_rows():
        for copy in own[2:]:
            copy.wait()
        deltas = []
        for h in range(HEADS):
            lanes = slice(h * SUB, (h + 1) * SUB)
            product = o_in[:, lanes].astype(F32) * mine[SUB : 2 * SUB, lanes].astype(F32)
            deltas.append(jnp.sum(product.T, axis=0, keepdims=True))
        zero = jnp.zeros((2, SUB), BF16)
        for h in range(HEADS):
            lse_parts = pieces(lse_in[h : h + 1, :] * (-1.0 / SCALE))
            delta_parts = pieces(-deltas[h])
            mine[2 * SUB : 2 * SUB + 16, h * SUB : (h + 1) * SUB] = jnp.concatenate(
                lse_parts + delta_parts + [zero] * 5, axis=0
            )

    def send_stats():
        for d in (1, 3, 2):
            q_rows[d].append(rows.start(mine.at[s_part], rows_in.at[core, y, s_part], me.at(dy=d)))
        mirrored[0] = pair.start(mine, rows_in.at[core, y], sibling)

    def relay():
        q_rows[1][0].wait_recv()
        block = rows_in.at[core, me.ys(-1), q_part]
        q_rows[2].append(rows.start(block, block, me.at(dy=1)))
        q_rows[3][0].wait_recv()
        block = rows_in.at[core, me.ys(1), g_part]
        q_rows[2].append(rows.start(block, block, me.at(dy=-1)))

    def mirror(d):
        for copy in q_rows[d] if d == 2 else q_rows[d][1:]:
            copy.wait_recv()
        block = rows_in.at[core, me.ys(-d)]
        mirrored[d] = pair.start(block, block, sibling)

    lane, low_cu, high_cu = doc_bounds(cu_ref)
    sub = lax.broadcasted_iota(jnp.int32, (SUB, 1), 0)

    def stack(d):
        mirrored[d].wait_recv()
        a = me.ys(-d)
        for c in range(2):
            row = x * 4 + z // 4 * 2 + c
            qpos = (a * 16 + row) * TILE + z % 4 * SUB + sub
            inside = (qpos >= low_cu) & (qpos < high_cu)
            doc_feat = jnp.where(inside | (lane < 16) | (lane >= 22), 0.0, -16384.0)
            for h in range(HEADS):
                lanes = slice(h * SUB, (h + 1) * SUB)
                to = slice(c * COLS + h * SUB, c * COLS + (h + 1) * SUB)
                qs[a, to, 0:128] = rows_in[c, a, 0:SUB, lanes]
                gs[a, to, 0:128] = rows_in[c, a, SUB : 2 * SUB, lanes]
                stat = rows_in[c, a, 2 * SUB : 2 * SUB + 16, lanes].astype(F32)
                stat = jnp.concatenate([stat, jnp.zeros((SUB - 16, SUB), F32)], axis=0).T
                lse_feat = jnp.where(lane < 3, stat, 0.0)
                delta_feat = jnp.where((lane >= 3) & (lane < 6), stat, 0.0)
                qs[a, to, 128:256] = (lse_feat + doc_feat).astype(BF16)
                gs[a, to, 128:256] = delta_feat.astype(BF16)

    i0 = x * 4 + z // 4 * 2
    zl = z % 4
    ones = lane < 6

    def key_base(b, jj):
        return (b * 16 + 4 * y + jj) * TILE + core * SUB

    def make_feats(kt, carry):
        for zh in range(2):
            pos = key_base(kt // 4, kt % 4) + zh * 2 * SUB + sub
            feats[kt, zh * SUB : (zh + 1) * SUB, :] = (
                (((pos >= low_cu) & (pos < high_cu)) | ones).astype(F32).astype(BF16)
            )
        return carry

    make_rows()
    send_stats()
    stack_own = pltpu.make_async_copy(mine, rows_in.at[core, y], own_sem.at[6])
    stack_own.start()
    k_first()
    v_step(1)
    relay()
    lax.fori_loop(0, 16, make_feats, 0)
    dqa[...] = jnp.zeros_like(dqa)
    v_step(2)
    v_step(3)
    v_step(4)
    mirror(1)
    mirror(3)
    k_step(1)
    stack_own.wait()
    stack(0)
    mirror(2)
    stack(1)
    stack(3)
    k_step(2)
    stack(2)
    own[1].wait()

    def k_last(n):
        block = ka.at[halves[n], me.zs(-3 if n == 0 else 3)]
        return pltpu.make_async_remote_copy(
            src_ref=block,
            dst_ref=block,
            send_sem=send_all.at[3],
            recv_sem=recv_k.at[12 + n],
            device_id=me.at(dz=1 if n == 0 else -1),
            device_id_type=MESH,
        )

    def k_third():
        for n in range(2):
            k_up[n].wait_recv()
            k_down[n].wait_recv()
            k_last(n).start()

    def k_fourth():
        for n in range(2):
            k_last(n).wait_recv()

    def cross_wait(n, first, last):
        for d in (1, 3, 2):
            whole = cross[d, n].copy(va.at[x, first:last], va.at[me.xs(-d), first:last], me.at(dx=d))
            whole.wait_recv()

    def tile_step(t, carry):
        g = t // 4
        n = (2 + g) % 4
        dx = (t + 1) % 4
        b = (x + dx) % 4
        jj = (zl + n) % 4
        kt = b * 4 + jj

        @pl.when(t == 0)
        def _():
            cross_wait(2, 3, 5)

        @pl.when(t == 2)
        def _():
            k_third()

        @pl.when(t == 4)
        def _():
            cross_wait(1, 1, 3)
            cross_wait(3, 5, 7)

        @pl.when(t == 8)
        def _():
            k_fourth()
            cross_wait(0, 0, 1)
            cross_wait(4, 7, 8)

        near = 2 * n - 1 + (3 - n) // 3
        far = 8 - 2 * n - n // 4
        far = far - (3 - n) // 3
        swap = (z + n) % 8 // 4
        v_first = near + (far - near) * swap
        v_second = far + (near - far) * swap
        keys = ka[b, pl.ds(2 * jj, 2)].reshape(2 * SUB, HEAD_DIM)
        vals = jnp.concatenate([va[b, v_first], va[b, v_second]], axis=0)
        own_tile = t % 4 // 3
        slot = 4 + (g - 4) * own_tile
        r = 4 * y + jj - i0
        acc[slot] = jnp.zeros((2, 2 * SUB, HEAD_DIM), F32)

        def unit(a, count, masked):
            wide = count * 2 * COLS
            many = pl.ds(a, count)
            feat = feats[kt]
            scores = lax.dot_general(
                jnp.concatenate([keys, feat], axis=1),
                qs[many].reshape(wide, 2 * HEAD_DIM),
                LANE,
                preferred_element_type=F32,
            )
            weights = jnp.exp2(scores * (SCALE * LOG2E))
            if masked:
                first = (a * 16 + i0) * TILE + zl * SUB
                kpos = lax.broadcasted_iota(jnp.int32, (2 * SUB, SUB), 0)
                kpos = jnp.where(kpos >= SUB, kpos + SUB, kpos) + key_base(b, jj)
                keep = [kpos <= first + lane, kpos <= first + TILE + lane]
                weights = jnp.concatenate(
                    [
                        jnp.where(keep[m // HEADS], weights[:, m * SUB : (m + 1) * SUB], 0.0)
                        for m in range(2 * HEADS)
                    ],
                    axis=1,
                )
            probs = lax.dot_general(
                jnp.concatenate([vals, feat], axis=1),
                gs[many].reshape(wide, 2 * HEAD_DIM),
                LANE,
                preferred_element_type=F32,
            )
            dscores = (weights * probs).astype(BF16)
            weights = weights.astype(BF16)
            g_rows = gs[many, :, 0:HEAD_DIM].reshape(wide, HEAD_DIM)
            q_all = qs[many, :, 0:HEAD_DIM].reshape(wide, HEAD_DIM)
            acc[slot, 0] += jnp.dot(dscores, q_all, preferred_element_type=F32)
            acc[slot, 1] += jnp.dot(weights, g_rows, preferred_element_type=F32)
            for m in range(count):
                dqa[a + m] += lax.dot_general(
                    keys,
                    dscores[:, m * 2 * COLS : (m + 1) * 2 * COLS],
                    ROW,
                    preferred_element_type=F32,
                )

        def half_unit(a):
            feat = feats[kt]
            q_half = qs[a, COLS : 2 * COLS]
            g_half = gs[a, COLS : 2 * COLS]
            scores = lax.dot_general(
                jnp.concatenate([keys, feat], axis=1), q_half, LANE, preferred_element_type=F32
            )
            weights = jnp.exp2(scores * (SCALE * LOG2E))
            kpos = lax.broadcasted_iota(jnp.int32, (2 * SUB, SUB), 0)
            kpos = jnp.where(kpos >= SUB, kpos + SUB, kpos)
            keep = kpos + core * SUB <= zl * SUB + lane
            weights = jnp.concatenate(
                [jnp.where(keep, weights[:, m * SUB : (m + 1) * SUB], 0.0) for m in range(HEADS)],
                axis=1,
            )
            probs = lax.dot_general(
                jnp.concatenate([vals, feat], axis=1), g_half, LANE, preferred_element_type=F32
            )
            dscores = (weights * probs).astype(BF16)
            weights = weights.astype(BF16)
            acc[slot, 0] += jnp.dot(dscores, q_half[:, 0:HEAD_DIM], preferred_element_type=F32)
            acc[slot, 1] += jnp.dot(weights, g_half[:, 0:HEAD_DIM], preferred_element_type=F32)
            dqa[a, :, COLS : 2 * COLS] += lax.dot_general(
                keys, dscores, ROW, preferred_element_type=F32
            )

        ahead = (r >= 0).astype(jnp.int32)
        start = b + ahead

        @pl.when(start <= 2)
        def _():
            unit(start, 2, False)

        def single(u, carry):
            unit(jnp.where(u == 0, 3, b), 1, True)
            return carry

        lax.fori_loop(jnp.where(start == 3, 0, 1), jnp.where(r == 0, 2, 1), single, 0)

        @pl.when(r == 1)
        def _():
            half_unit(b)

        @pl.when(own_tile == 0)
        def _():
            for zh in range(2):
                part = slice(zh * SUB, (zh + 1) * SUB)
                stage[t, zh, 0] = (acc[4, 0, part] * SCALE).astype(BF16)
                stage[t, zh, 1] = acc[4, 1, part].astype(BF16)
            side_copy(t, dx).start()

        @pl.when((t > 4) & (t % 4 == 3))
        def _():
            z_start(g - 1)

        return carry

    def side_copy(t, dx):
        return pltpu.make_async_remote_copy(
            src_ref=stage.at[t],
            dst_ref=side_in.at[t],
            send_sem=send_s.at[t],
            recv_sem=recv_s.at[t],
            device_id=me.at(dx=dx),
            device_id_type=MESH,
        )

    def z_copy(g, dz):
        return pltpu.make_async_remote_copy(
            src_ref=z_send.at[g, (z + dz) % 8 // 4],
            dst_ref=z_in.at[dz],
            send_sem=send_z.at[dz],
            recv_sem=recv_z.at[dz],
            device_id=me.at(dz=dz),
            device_id_type=MESH,
        )

    def z_start(g):
        n = (2 + g) % 4
        for e in range(3):
            side_copy(4 * g + e, e + 1).wait_recv()
        for zh in range(2):
            part = slice(zh * SUB, (zh + 1) * SUB)
            for kv in range(2):
                total = acc[g, kv, part] * (SCALE if kv == 0 else 1.0)
                for e in range(3):
                    total += side_in[4 * g + e, zh, kv].astype(F32)
                z_send[g, zh, kv] = total.astype(BF16)

        @pl.when(n > 0)
        def _():
            z_copy(g, n).start()

        z_copy(g, n + 4).start()

    lax.fori_loop(0, 16, tile_step, 0)

    last = Sender(send_d, recv_d)
    swaps = {}

    def dq_swap(d):
        a = me.ys(d)
        for c in range(2):
            for h in range(HEADS):
                lanes = slice(h * SUB, (h + 1) * SUB)
                to = slice(c * COLS + h * SUB, c * COLS + (h + 1) * SUB)
                dq_low[c, a, :, lanes] = (dqa[a, :, to].T * SCALE).astype(BF16)
        swaps[d] = last.start(dq_low.at[1 - core, a], q_pair.at[a], sibling)

    q_back = []

    def dq_send(d):
        a = me.ys(d)
        swaps[d].wait_recv()
        q_send[d - 1] = (dq_low[core, a].astype(F32) + q_pair[a].astype(F32)).astype(BF16)
        q_back.append(last.start(q_send.at[d - 1], q_in.at[d - 1], me.at(dy=d)))

    dq_swap(2)
    dq_swap(1)
    dq_swap(3)
    dq_send(2)
    dq_send(1)
    dq_send(3)
    z_start(3)
    dq_swap(0)
    swaps[0].wait_recv()
    for dz in (2, 6, 3, 7, 4, 1, 5):
        z_copy((dz + 2) % 4, dz).wait_recv()
    for kv in range(2):
        total = z_send[2, z // 4, kv].astype(F32)
        for dz in range(1, 8):
            total += z_in[dz, kv].astype(F32)
        lanes = slice(COLS + kv * HEAD_DIM, COLS + (kv + 1) * HEAD_DIM)
        all_out[:, lanes] = total.astype(BF16)
    total = dq_low[core, y].astype(F32) + q_pair[y].astype(F32)
    for copy in q_back:
        copy.wait_recv()
    for m in range(3):
        total += q_in[m].astype(F32)
    all_out[:, 0:COLS] = total.astype(BF16)

    rows.finish(rows_in.at[0, 0:3], sibling)
    pair.finish(rows_in.at[0], sibling)
    v_ring.finish(va.at[x, 0:7], sibling)
    k_ring.finish(ka.at[0:4, 0:7], sibling)
    k_cross.finish()
    for n, first, size in ((0, 0, 1), (1, 1, 2), (2, 3, 2), (3, 5, 2), (4, 7, 1)):
        for d in (1, 2, 3):
            block = va.at[x, first : first + size]
            cross[d, n].copy(block, block, me.at(dx=d)).wait_send()
    for g in range(4):
        for e in range(3):
            side_copy(4 * g + e, e + 1).wait_send()
    for dz in range(1, 8):
        z_copy((dz + 2) % 4, dz).wait_send()
    last.finish()


def grads(cu, q, g, k, v, o, lse):
    dma = pltpu.SemaphoreType.DMA
    block = (SUB, HEAD_DIM)
    message = (2 * SUB + 16, COLS)
    vmem = pltpu.VMEM
    return pl.pallas_call(
        grads_kernel,
        out_shape=jax.ShapeDtypeStruct((SUB, COLS + 2 * HEAD_DIM), BF16),
        in_specs=[pl.BlockSpec(memory_space=pltpu.SMEM)] + [ANY] * 6,
        out_specs=VMEM,
        scratch_shapes=[
            vmem((4, 8) + block, BF16),
            vmem((4, 8) + block, BF16),
            vmem((2, 4) + message, BF16),
            vmem(message, BF16),
            vmem((4, 2 * COLS, 2 * HEAD_DIM), BF16),
            vmem((4, 2 * COLS, 2 * HEAD_DIM), BF16),
            vmem((SUB, COLS), BF16),
            vmem((HEADS, SUB), F32),
            vmem((16, 2 * SUB, HEAD_DIM), BF16),
            vmem((5, 2, 2 * SUB, HEAD_DIM), F32),
            vmem((4, HEAD_DIM, 2 * COLS), F32),
            vmem((16, 2, 2) + block, BF16),
            vmem((16, 2, 2) + block, BF16),
            vmem((4, 2, 2) + block, BF16),
            vmem((8, 2) + block, BF16),
            vmem((2, 4, SUB, COLS), BF16),
            vmem((4, SUB, COLS), BF16),
            vmem((3, SUB, COLS), BF16),
            vmem((3, SUB, COLS), BF16),
            dma((9,)),
            dma((4,)),
            dma((8,)),
            dma((14,)),
            dma((3, 5)),
            dma((3, 5)),
            dma((3,)),
            dma((3,)),
            dma((4,)),
            dma((7,)),
            dma((16,)),
            dma((16,)),
            dma((8,)),
            dma((8,)),
            dma((7,)),
            dma((7,)),
        ],
        compiler_params=pltpu.CompilerParams(
            collective_id=0, has_side_effects=True, vmem_limit_bytes=63 * 1024 * 1024
        ),
        name="grads",
    )(cu, q, g, k, v, o, lse)


def split_kernel(all_ref, dq_ref, dk_ref, dv_ref):
    dq_ref[...] = all_ref[:, 0:COLS]
    dk_ref[...] = all_ref[:, COLS : COLS + HEAD_DIM]
    dv_ref[...] = all_ref[:, COLS + HEAD_DIM : COLS + 2 * HEAD_DIM]


def split(grads):
    return pl.pallas_call(
        split_kernel,
        out_shape=[
            jax.ShapeDtypeStruct((SUB, COLS), BF16),
            jax.ShapeDtypeStruct((SUB, HEAD_DIM), BF16),
            jax.ShapeDtypeStruct((SUB, HEAD_DIM), BF16),
        ],
        in_specs=[VMEM],
        out_specs=[VMEM] * 3,
        name="split",
    )(grads)


def per_device(query, keys, values, out, out_grad, lse, cu_seqlens, tile_table):
    return split(grads(cu_seqlens, query, out_grad, keys, values, out, lse))


def solution(mesh):
    placed = (
        P(("qrow", "kcol"), None),
        P(("kcol", "qrow"), None),
        P(("kcol", "qrow"), None),
        P(("qrow", "kcol"), None),
        P(("qrow", "kcol"), None),
        P(None, ("qrow", "kcol")),
        P(),
        P("qrow", "kcol", None),
    )
    return jax.shard_map(
        per_device,
        mesh=mesh,
        in_specs=placed,
        out_specs=(P(("qrow", "kcol"), None), P(("kcol", "qrow"), None), P(("kcol", "qrow"), None)),
        check_vma=False,
    )
```

```python
import math

import jax
import jax.numpy as jnp
from jax import lax
from jax.experimental import pallas as pl
from jax.experimental.pallas import tpu as pltpu
from jax.sharding import PartitionSpec as P

MESH = pl.DeviceIdType.MESH
HEADS = 4
HEAD_DIM = 128
TILE = 512
SUB = 128
COLS = HEADS * SUB
TOKENS = 32768
SCALE = 1.0 / math.sqrt(HEAD_DIM)
LOG2E = math.log2(math.e)
LANE = (((1,), (1,)), ((), ()))
ROW = (((0,), (0,)), ((), ()))
BF16 = jnp.bfloat16
F32 = jnp.float32
VMEM = pl.BlockSpec(memory_space=pltpu.VMEM)
ANY = pl.BlockSpec(memory_space=pl.ANY)


class Place:
    def __init__(self):
        row = lax.axis_index("qrow")
        col = lax.axis_index("kcol")
        self.x = row // 4
        self.core = row % 2
        self.y = col // 4
        self.z = row // 2 % 2 * 4 + col % 4

    def at(self, dx=0, dy=0, dz=0, flip=0):
        x = (self.x + dx + 4) % 4
        y = (self.y + dy + 4) % 4
        z = (self.z + dz + 8) % 8
        core = 1 - self.core if flip else self.core
        return (x * 4 + z // 4 * 2 + core, y * 4 + z % 4)

    def xs(self, dx):
        return (self.x + dx + 4) % 4

    def ys(self, dy):
        return (self.y + dy + 4) % 4

    def zs(self, dz):
        z = (self.z + dz + 8) % 8
        return z % 4 * 2 + z // 4


class Sender:
    def __init__(self, send_sem, recv_sem):
        self.send_sem = send_sem
        self.recv_sem = recv_sem
        self.sent = []

    def start(self, src, dst, device):
        number = len(self.sent)
        copy = pltpu.make_async_remote_copy(
            src_ref=src,
            dst_ref=dst,
            send_sem=self.send_sem.at[number],
            recv_sem=self.recv_sem.at[number],
            device_id=device,
            device_id_type=MESH,
        )
        copy.start()
        self.sent.append(copy)
        return copy

    def finish(self):
        for copy in self.sent:
            copy.wait_send()


def greet(devices):
    barrier = pltpu.get_barrier_semaphore()
    for device in devices:
        pl.semaphore_signal(barrier, inc=1, device_id=device, device_id_type=MESH)
    pl.semaphore_wait(barrier, len(devices))


def load(pairs, sems):
    copies = [pltpu.make_async_copy(src, dst, sems.at[n]) for n, (src, dst) in enumerate(pairs)]
    for copy in copies:
        copy.start()
    return copies


def doc_bounds(cu_ref):
    lane = lax.broadcasted_iota(jnp.int32, (1, SUB), 1)
    low = jnp.zeros((1, SUB), jnp.int32) + TOKENS
    high = jnp.zeros((1, SUB), jnp.int32)
    for n in range(6):
        low = jnp.where(lane == 16 + n, cu_ref[n], low)
        high = jnp.where(lane == 16 + n, cu_ref[n + 1], high)
    return lane, low, high


def pieces(vec):
    out = []
    for n in range(3):
        piece = vec.astype(BF16)
        vec = vec - piece.astype(F32)
        out.append(piece)
    return out


def spot(dz):
    if abs(dz) == 4:
        return 7
    return 0 if dz == 0 else 2 * abs(dz) - (1 if dz > 0 else 0)


class Batch:
    def __init__(self, send_sem, recv_sem):
        self.send_sem = send_sem
        self.recv_sem = recv_sem

    def copy(self, src, dst, device):
        return pltpu.make_async_remote_copy(
            src_ref=src,
            dst_ref=dst,
            send_sem=self.send_sem,
            recv_sem=self.recv_sem,
            device_id=device,
            device_id_type=MESH,
        )

    def start(self, src, dst, device):
        self.copy(src, dst, device).start()


class Lane(Sender):
    def __init__(self, send_sem, recv_sem):
        super().__init__(send_sem, recv_sem)

    def start(self, src, dst, device):
        copy = pltpu.make_async_remote_copy(
            src_ref=src,
            dst_ref=dst,
            send_sem=self.send_sem,
            recv_sem=self.recv_sem.at[len(self.sent)],
            device_id=device,
            device_id_type=MESH,
        )
        copy.start()
        self.sent.append(copy)
        return copy

    def finish(self, whole, device):
        pltpu.make_async_remote_copy(
            src_ref=whole,
            dst_ref=whole,
            send_sem=self.send_sem,
            recv_sem=self.recv_sem.at[0],
            device_id=device,
            device_id_type=MESH,
        ).wait_send()


def grads_kernel(
    cu_ref, q_ref, g_ref, k_ref, v_ref, o_ref, lse_ref, all_out, ka, va, rows_in, mine, qs, gs, o_in, lse_in, feats, acc, dqa,
    stage, side_in, z_send, z_in, dq_low, q_pair, q_send, q_in,
    recv_q, recv_m, recv_v, recv_k, send_x, recv_x, send_k, recv_kx, send_all, own_sem, send_s, recv_s, send_z, recv_z, send_d, recv_d
):
    me = Place()
    x, y, z, core = me.x, me.y, me.z, me.core
    here = me.zs(0)
    sibling = me.at(flip=1)
    own = load(
        [
            (k_ref, ka.at[x, here]),
            (v_ref, va.at[x, 0]),
            (q_ref, mine.at[0:SUB]),
            (g_ref, mine.at[SUB : 2 * SUB]),
            (o_ref, o_in),
            (lse_ref, lse_in),
        ],
        own_sem,
    )
    greet(
        [me.at(dx=d) for d in (1, 2, 3)]
        + [me.at(dy=d) for d in (1, 2, 3)]
        + [me.at(dz=d) for d in range(1, 8)]
        + [sibling]
    )
    rows = Lane(send_all.at[0], recv_q)
    pair = Lane(send_all.at[1], recv_m)
    v_ring = Lane(send_all.at[2], recv_v)
    k_ring = Lane(send_all.at[3], recv_k)
    k_cross = Sender(send_k, recv_kx)
    q_part, g_part, s_part = slice(0, SUB), slice(SUB, 2 * SUB), slice(2 * SUB, 2 * SUB + 16)
    mirrored = {}
    q_rows = {1: [], 2: [], 3: []}

    def send_rows():
        for n in range(2):
            for d, part, src in ((1, q_part, q_ref), (3, g_part, g_ref)) if n == 0 else (
                (1, g_part, g_ref),
                (3, q_part, q_ref),
            ):
                q_rows[d].append(rows.start(src, rows_in.at[core, y, part], me.at(dy=d)))

    cross = {(d, n): Batch(send_x.at[d - 1, n], recv_x.at[d - 1, n]) for d in (1, 2, 3) for n in range(5)}
    send_rows()
    k_side = [k_cross.start(k_ref, ka.at[x, here], me.at(dx=d)) for d in (2, 1, 3)]
    v_in = {d: v_ring.start(v_ref, va.at[x, spot(-d)], me.at(dz=d)) for d in (1, -1, 2, -2, 3, -3, 4)}
    for d in (2, 1, 3):
        cross[d, 0].start(v_ref, va.at[x, 0], me.at(dx=d))

    def spread(first, last):
        block = va.at[x, first:last]
        for d in (2, 1, 3):
            cross[d, (first + 1) // 2].start(block, block, me.at(dx=d))

    halves = (slice(0, 2), slice(2, 4))
    k_up = []
    k_down = []

    def k_first():
        own[0].wait()
        for copy in k_side:
            copy.wait_recv()
        for half in halves:
            block = ka.at[half, here]
            k_up.append(k_ring.start(block, block, me.at(dz=1)))
            k_down.append(k_ring.start(block, block, me.at(dz=-1)))

    def k_step(step):
        for n, half in enumerate(halves):
            k_up[n].wait_recv()
            block = ka.at[half, me.zs(-step)]
            k_up[n] = k_ring.start(block, block, me.at(dz=1))
            k_down[n].wait_recv()
            block = ka.at[half, me.zs(step)]
            k_down[n] = k_ring.start(block, block, me.at(dz=-1))

    def v_step(step):
        v_in[step].wait_recv()
        if step < 4:
            v_in[-step].wait_recv()
            spread(2 * step - 1, 2 * step + 1)
        else:
            spread(7, 8)

    def make_rows():
        for copy in own[2:]:
            copy.wait()
        deltas = []
        for h in range(HEADS):
            lanes = slice(h * SUB, (h + 1) * SUB)
            product = o_in[:, lanes].astype(F32) * mine[SUB : 2 * SUB, lanes].astype(F32)
            deltas.append(jnp.sum(product.T, axis=0, keepdims=True))
        zero = jnp.zeros((2, SUB), BF16)
        for h in range(HEADS):
            lse_parts = pieces(lse_in[h : h + 1, :] * (-1.0 / SCALE))
            delta_parts = pieces(-deltas[h])
            mine[2 * SUB : 2 * SUB + 16, h * SUB : (h + 1) * SUB] = jnp.concatenate(
                lse_parts + delta_parts + [zero] * 5, axis=0
            )

    def send_stats():
        for d in (1, 3, 2):
            q_rows[d].append(rows.start(mine.at[s_part], rows_in.at[core, y, s_part], me.at(dy=d)))
        mirrored[0] = pair.start(mine, rows_in.at[core, y], sibling)

    def relay():
        q_rows[1][0].wait_recv()
        block = rows_in.at[core, me.ys(-1), q_part]
        q_rows[2].append(rows.start(block, block, me.at(dy=1)))
        q_rows[3][0].wait_recv()
        block = rows_in.at[core, me.ys(1), g_part]
        q_rows[2].append(rows.start(block, block, me.at(dy=-1)))

    def mirror(d):
        for copy in q_rows[d] if d == 2 else q_rows[d][1:]:
            copy.wait_recv()
        block = rows_in.at[core, me.ys(-d)]
        mirrored[d] = pair.start(block, block, sibling)

    lane, low_cu, high_cu = doc_bounds(cu_ref)
    sub = lax.broadcasted_iota(jnp.int32, (SUB, 1), 0)

    def stack(d):
        mirrored[d].wait_recv()
        a = me.ys(-d)
        for c in range(2):
            row = x * 4 + z // 4 * 2 + c
            qpos = (a * 16 + row) * TILE + z % 4 * SUB + sub
            inside = (qpos >= low_cu) & (qpos < high_cu)
            doc_feat = jnp.where(inside | (lane < 16) | (lane >= 22), 0.0, -16384.0)
            for h in range(HEADS):
                lanes = slice(h * SUB, (h + 1) * SUB)
                to = slice(c * COLS + h * SUB, c * COLS + (h + 1) * SUB)
                qs[a, to, 0:128] = rows_in[c, a, 0:SUB, lanes]
                gs[a, to, 0:128] = rows_in[c, a, SUB : 2 * SUB, lanes]
                stat = rows_in[c, a, 2 * SUB : 2 * SUB + 16, lanes].astype(F32)
                stat = jnp.concatenate([stat, jnp.zeros((SUB - 16, SUB), F32)], axis=0).T
                lse_feat = jnp.where(lane < 3, stat, 0.0)
                delta_feat = jnp.where((lane >= 3) & (lane < 6), stat, 0.0)
                qs[a, to, 128:256] = (lse_feat + doc_feat).astype(BF16)
                gs[a, to, 128:256] = delta_feat.astype(BF16)

    i0 = x * 4 + z // 4 * 2
    zl = z % 4
    ones = lane < 6

    def key_base(b, jj):
        return (b * 16 + 4 * y + jj) * TILE + core * SUB

    def make_feats(kt, carry):
        for zh in range(2):
            pos = key_base(kt // 4, kt % 4) + zh * 2 * SUB + sub
            feats[kt, zh * SUB : (zh + 1) * SUB, :] = (
                (((pos >= low_cu) & (pos < high_cu)) | ones).astype(F32).astype(BF16)
            )
        return carry

    make_rows()
    send_stats()
    stack_own = pltpu.make_async_copy(mine, rows_in.at[core, y], own_sem.at[6])
    stack_own.start()
    k_first()
    v_step(1)
    relay()
    lax.fori_loop(0, 16, make_feats, 0)
    dqa[...] = jnp.zeros_like(dqa)
    v_step(2)
    v_step(3)
    v_step(4)
    mirror(1)
    mirror(3)
    k_step(1)
    stack_own.wait()
    stack(0)
    mirror(2)
    stack(1)
    stack(3)
    k_step(2)
    stack(2)
    own[1].wait()

    def k_last(n):
        block = ka.at[halves[n], me.zs(-3 if n == 0 else 3)]
        return pltpu.make_async_remote_copy(
            src_ref=block,
            dst_ref=block,
            send_sem=send_all.at[3],
            recv_sem=recv_k.at[12 + n],
            device_id=me.at(dz=1 if n == 0 else -1),
            device_id_type=MESH,
        )

    def k_third():
        for n in range(2):
            k_up[n].wait_recv()
            k_down[n].wait_recv()
            k_last(n).start()

    def k_fourth():
        for n in range(2):
            k_last(n).wait_recv()

    def cross_wait(n, first, last):
        for d in (1, 3, 2):
            whole = cross[d, n].copy(va.at[x, first:last], va.at[me.xs(-d), first:last], me.at(dx=d))
            whole.wait_recv()

    def tile_step(t, carry):
        g = t // 4
        n = (2 + g) % 4
        dx = (t + 1) % 4
        b = (x + dx) % 4
        jj = (zl + n) % 4
        kt = b * 4 + jj

        @pl.when(t == 0)
        def _():
            cross_wait(2, 3, 5)

        @pl.when(t == 2)
        def _():
            k_third()

        @pl.when(t == 4)
        def _():
            cross_wait(1, 1, 3)
            cross_wait(3, 5, 7)

        @pl.when(t == 8)
        def _():
            k_fourth()
            cross_wait(0, 0, 1)
            cross_wait(4, 7, 8)

        near = 2 * n - 1 + (3 - n) // 3
        far = 8 - 2 * n - n // 4
        far = far - (3 - n) // 3
        swap = (z + n) % 8 // 4
        v_first = near + (far - near) * swap
        v_second = far + (near - far) * swap
        keys = ka[b, pl.ds(2 * jj, 2)].reshape(2 * SUB, HEAD_DIM)
        vals = jnp.concatenate([va[b, v_first], va[b, v_second]], axis=0)
        own_tile = t % 4 // 3
        slot = 4 + (g - 4) * own_tile
        r = 4 * y + jj - i0
        acc[slot] = jnp.zeros((2, 2 * SUB, HEAD_DIM), F32)

        def unit(a, count, masked):
            wide = count * 2 * COLS
            many = pl.ds(a, count)
            feat = feats[kt]
            scores = lax.dot_general(
                jnp.concatenate([keys, feat], axis=1),
                qs[many].reshape(wide, 2 * HEAD_DIM),
                LANE,
                preferred_element_type=F32,
            )
            weights = jnp.exp2(scores * (SCALE * LOG2E))
            if masked:
                first = (a * 16 + i0) * TILE + zl * SUB
                kpos = lax.broadcasted_iota(jnp.int32, (2 * SUB, SUB), 0)
                kpos = jnp.where(kpos >= SUB, kpos + SUB, kpos) + key_base(b, jj)
                keep = [kpos <= first + lane, kpos <= first + TILE + lane]
                weights = jnp.concatenate(
                    [
                        jnp.where(keep[m // HEADS], weights[:, m * SUB : (m + 1) * SUB], 0.0)
                        for m in range(2 * HEADS)
                    ],
                    axis=1,
                )
            probs = lax.dot_general(
                jnp.concatenate([vals, feat], axis=1),
                gs[many].reshape(wide, 2 * HEAD_DIM),
                LANE,
                preferred_element_type=F32,
            )
            dscores = (weights * probs).astype(BF16)
            weights = weights.astype(BF16)
            g_rows = gs[many, :, 0:HEAD_DIM].reshape(wide, HEAD_DIM)
            q_all = qs[many, :, 0:HEAD_DIM].reshape(wide, HEAD_DIM)
            acc[slot, 0] += jnp.dot(dscores, q_all, preferred_element_type=F32)
            acc[slot, 1] += jnp.dot(weights, g_rows, preferred_element_type=F32)
            for m in range(count):
                dqa[a + m] += lax.dot_general(
                    keys,
                    dscores[:, m * 2 * COLS : (m + 1) * 2 * COLS],
                    ROW,
                    preferred_element_type=F32,
                )

        def half_unit(a):
            feat = feats[kt]
            q_half = qs[a, COLS : 2 * COLS]
            g_half = gs[a, COLS : 2 * COLS]
            scores = lax.dot_general(
                jnp.concatenate([keys, feat], axis=1), q_half, LANE, preferred_element_type=F32
            )
            weights = jnp.exp2(scores * (SCALE * LOG2E))
            kpos = lax.broadcasted_iota(jnp.int32, (2 * SUB, SUB), 0)
            kpos = jnp.where(kpos >= SUB, kpos + SUB, kpos)
            keep = kpos + core * SUB <= zl * SUB + lane
            weights = jnp.concatenate(
                [jnp.where(keep, weights[:, m * SUB : (m + 1) * SUB], 0.0) for m in range(HEADS)],
                axis=1,
            )
            probs = lax.dot_general(
                jnp.concatenate([vals, feat], axis=1), g_half, LANE, preferred_element_type=F32
            )
            dscores = (weights * probs).astype(BF16)
            weights = weights.astype(BF16)
            acc[slot, 0] += jnp.dot(dscores, q_half[:, 0:HEAD_DIM], preferred_element_type=F32)
            acc[slot, 1] += jnp.dot(weights, g_half[:, 0:HEAD_DIM], preferred_element_type=F32)
            dqa[a, :, COLS : 2 * COLS] += lax.dot_general(
                keys, dscores, ROW, preferred_element_type=F32
            )

        ahead = (r >= 0).astype(jnp.int32)
        start = b + ahead

        @pl.when(start <= 2)
        def _():
            unit(start, 2, False)

        def single(u, carry):
            unit(jnp.where(u == 0, 3, b), 1, True)
            return carry

        lax.fori_loop(jnp.where(start == 3, 0, 1), jnp.where(r == 0, 2, 1), single, 0)

        @pl.when(r == 1)
        def _():
            half_unit(b)

        @pl.when(own_tile == 0)
        def _():
            for zh in range(2):
                part = slice(zh * SUB, (zh + 1) * SUB)
                stage[t, zh, 0] = (acc[4, 0, part] * SCALE).astype(BF16)
                stage[t, zh, 1] = acc[4, 1, part].astype(BF16)
            side_copy(t, dx).start()

        @pl.when((t > 4) & (t % 4 == 3))
        def _():
            z_start(g - 1)

        return carry

    def side_copy(t, dx):
        return pltpu.make_async_remote_copy(
            src_ref=stage.at[t],
            dst_ref=side_in.at[t],
            send_sem=send_s.at[t],
            recv_sem=recv_s.at[t],
            device_id=me.at(dx=dx),
            device_id_type=MESH,
        )

    def z_copy(g, dz):
        return pltpu.make_async_remote_copy(
            src_ref=z_send.at[g, (z + dz) % 8 // 4],
            dst_ref=z_in.at[dz],
            send_sem=send_z.at[dz],
            recv_sem=recv_z.at[dz],
            device_id=me.at(dz=dz),
            device_id_type=MESH,
        )

    def z_start(g):
        n = (2 + g) % 4
        for e in range(3):
            side_copy(4 * g + e, e + 1).wait_recv()
        for zh in range(2):
            part = slice(zh * SUB, (zh + 1) * SUB)
            for kv in range(2):
                total = acc[g, kv, part] * (SCALE if kv == 0 else 1.0)
                for e in range(3):
                    total += side_in[4 * g + e, zh, kv].astype(F32)
                z_send[g, zh, kv] = total.astype(BF16)

        @pl.when(n > 0)
        def _():
            z_copy(g, n).start()

        z_copy(g, n + 4).start()

    lax.fori_loop(0, 16, tile_step, 0)

    last = Sender(send_d, recv_d)
    swaps = {}

    def dq_swap(d):
        a = me.ys(d)
        for c in range(2):
            for h in range(HEADS):
                lanes = slice(h * SUB, (h + 1) * SUB)
                to = slice(c * COLS + h * SUB, c * COLS + (h + 1) * SUB)
                dq_low[c, a, :, lanes] = (dqa[a, :, to].T * SCALE).astype(BF16)
        swaps[d] = last.start(dq_low.at[1 - core, a], q_pair.at[a], sibling)

    q_back = []

    def dq_send(d):
        a = me.ys(d)
        swaps[d].wait_recv()
        q_send[d - 1] = (dq_low[core, a].astype(F32) + q_pair[a].astype(F32)).astype(BF16)
        q_back.append(last.start(q_send.at[d - 1], q_in.at[d - 1], me.at(dy=d)))

    dq_swap(2)
    dq_swap(1)
    dq_swap(3)
    dq_send(2)
    z_start(3)
    dq_send(1)
    dq_send(3)
    dq_swap(0)
    swaps[0].wait_recv()
    for dz in (2, 6, 3, 7, 4, 1, 5):
        z_copy((dz + 2) % 4, dz).wait_recv()
    for kv in range(2):
        total = z_send[2, z // 4, kv].astype(F32)
        for dz in range(1, 8):
            total += z_in[dz, kv].astype(F32)
        lanes = slice(COLS + kv * HEAD_DIM, COLS + (kv + 1) * HEAD_DIM)
        all_out[:, lanes] = total.astype(BF16)
    total = dq_low[core, y].astype(F32) + q_pair[y].astype(F32)
    for copy in q_back:
        copy.wait_recv()
    for m in range(3):
        total += q_in[m].astype(F32)
    all_out[:, 0:COLS] = total.astype(BF16)

    rows.finish(rows_in.at[0, 0:3], sibling)
    pair.finish(rows_in.at[0], sibling)
    v_ring.finish(va.at[x, 0:7], sibling)
    k_ring.finish(ka.at[0:4, 0:7], sibling)
    k_cross.finish()
    for n, first, size in ((0, 0, 1), (1, 1, 2), (2, 3, 2), (3, 5, 2), (4, 7, 1)):
        for d in (1, 2, 3):
            block = va.at[x, first : first + size]
            cross[d, n].copy(block, block, me.at(dx=d)).wait_send()
    for g in range(4):
        for e in range(3):
            side_copy(4 * g + e, e + 1).wait_send()
    for dz in range(1, 8):
        z_copy((dz + 2) % 4, dz).wait_send()
    last.finish()


def grads(cu, q, g, k, v, o, lse):
    dma = pltpu.SemaphoreType.DMA
    block = (SUB, HEAD_DIM)
    message = (2 * SUB + 16, COLS)
    vmem = pltpu.VMEM
    return pl.pallas_call(
        grads_kernel,
        out_shape=jax.ShapeDtypeStruct((SUB, COLS + 2 * HEAD_DIM), BF16),
        in_specs=[pl.BlockSpec(memory_space=pltpu.SMEM)] + [ANY] * 6,
        out_specs=VMEM,
        scratch_shapes=[
            vmem((4, 8) + block, BF16),
            vmem((4, 8) + block, BF16),
            vmem((2, 4) + message, BF16),
            vmem(message, BF16),
            vmem((4, 2 * COLS, 2 * HEAD_DIM), BF16),
            vmem((4, 2 * COLS, 2 * HEAD_DIM), BF16),
            vmem((SUB, COLS), BF16),
            vmem((HEADS, SUB), F32),
            vmem((16, 2 * SUB, HEAD_DIM), BF16),
            vmem((5, 2, 2 * SUB, HEAD_DIM), F32),
            vmem((4, HEAD_DIM, 2 * COLS), F32),
            vmem((16, 2, 2) + block, BF16),
            vmem((16, 2, 2) + block, BF16),
            vmem((4, 2, 2) + block, BF16),
            vmem((8, 2) + block, BF16),
            vmem((2, 4, SUB, COLS), BF16),
            vmem((4, SUB, COLS), BF16),
            vmem((3, SUB, COLS), BF16),
            vmem((3, SUB, COLS), BF16),
            dma((9,)),
            dma((4,)),
            dma((8,)),
            dma((14,)),
            dma((3, 5)),
            dma((3, 5)),
            dma((3,)),
            dma((3,)),
            dma((4,)),
            dma((7,)),
            dma((16,)),
            dma((16,)),
            dma((8,)),
            dma((8,)),
            dma((7,)),
            dma((7,)),
        ],
        compiler_params=pltpu.CompilerParams(
            collective_id=0, has_side_effects=True, vmem_limit_bytes=63 * 1024 * 1024
        ),
        name="grads",
    )(cu, q, g, k, v, o, lse)


def split_kernel(all_ref, dq_ref, dk_ref, dv_ref):
    dq_ref[...] = all_ref[:, 0:COLS]
    dk_ref[...] = all_ref[:, COLS : COLS + HEAD_DIM]
    dv_ref[...] = all_ref[:, COLS + HEAD_DIM : COLS + 2 * HEAD_DIM]


def split(grads):
    return pl.pallas_call(
        split_kernel,
        out_shape=[
            jax.ShapeDtypeStruct((SUB, COLS), BF16),
            jax.ShapeDtypeStruct((SUB, HEAD_DIM), BF16),
            jax.ShapeDtypeStruct((SUB, HEAD_DIM), BF16),
        ],
        in_specs=[VMEM],
        out_specs=[VMEM] * 3,
        name="split",
    )(grads)


def per_device(query, keys, values, out, out_grad, lse, cu_seqlens, tile_table):
    return split(grads(cu_seqlens, query, out_grad, keys, values, out, lse))


def solution(mesh):
    placed = (
        P(("qrow", "kcol"), None),
        P(("kcol", "qrow"), None),
        P(("kcol", "qrow"), None),
        P(("qrow", "kcol"), None),
        P(("qrow", "kcol"), None),
        P(None, ("qrow", "kcol")),
        P(),
        P("qrow", "kcol", None),
    )
    return jax.shard_map(
        per_device,
        mesh=mesh,
        in_specs=placed,
        out_specs=(P(("qrow", "kcol"), None), P(("kcol", "qrow"), None), P(("kcol", "qrow"), None)),
        check_vma=False,
    )
```
